256 devices in a mesh: replica: 4 (over y), fsdp: 16 (over x, z_hi), tensor: 4 (over z_lo, core).
Axes of the slice: x: 4, y: 4, z: 8 (z_hi: 4, z_lo: 2; z = z_hi * 2 + z_lo), core: 2. Of those that a mesh axis runs over, the one named last changes fastest.
Arguments:
- hidden: bfloat16 [4, 8192, 4096], P('replica', ('fsdp', 'tensor')), may hold values from -6 to 6
- norm_gain: float32 [4096], replicated, may hold values from 0.5 to 3
- attn_weight: bfloat16 [4, 4096, 4, 1280], P('replica', 'fsdp', 'tensor'), may hold values from -0.09375 to 0.09375
- adam_first: float32 [4, 4096, 4, 1280], P('replica', 'fsdp', 'tensor'), may hold values from -6 to 6
- adam_second: float32 [4, 4096, 4, 1280], P('replica', 'fsdp', 'tensor'), may hold values from 1 to 100
- cotangent: bfloat16 [4, 8192, 4096], P('replica', ('fsdp', 'tensor')), may hold values from -6 to 6
- pseudo_grad: bfloat16 [4, 8388608], P('replica', ('fsdp', 'tensor')), may hold values from -6 to 6
- outer_params: float32 [8388608], P(('fsdp', 'tensor')), may hold values from -6 to 6
- outer_moment: float32 [8388608], P(('fsdp', 'tensor')), may hold values from -3 to 3
- inner_frag: bfloat16 [4, 8388608], P('replica', ('fsdp', 'tensor')), may hold values from -6 to 6
Outputs:
- layer_out: bfloat16 [4, 8192, 4096], P('replica', ('fsdp', 'tensor'))
- hidden_grad: bfloat16 [4, 8192, 4096], P('replica', ('fsdp', 'tensor'))
- new_weight: bfloat16 [4, 4096, 4, 1280], P('replica', 'fsdp', 'tensor')
- new_first: float32 [4, 4096, 4, 1280], P('replica', 'fsdp', 'tensor')
- new_second: float32 [4, 4096, 4, 1280], P('replica', 'fsdp', 'tensor')
- new_outer: float32 [8388608], P(('fsdp', 'tensor'))
- new_moment: float32 [8388608], P(('fsdp', 'tensor'))
- new_inner: bfloat16 [4, 8388608], P('replica', ('fsdp', 'tensor'))
The draws below stay inside these ranges and needn't reach their ends.
All inputs are finite; a program needn't handle non-finite values.
Results may differ from the reference program's by a relative error of at most 0.029.
Values may be sent and summed in bfloat16 or wider, within the bound.
No kernel may reach another device: no remote copies, remote signals or barrier semaphores. Data moves between devices by JAX's collectives and lax.ppermute only.
A program may use at most 128 MiB of HBM per device.

```python
import math
import jax
import jax.numpy as jnp
from jax import lax

D = 4096
HQ = 16
HK = 4
HD = 128
TOK_DEV = 512
PACK = 1280
TOKENS = 8192
FRAG = 8388608
N_REPLICA = 4
N_FSDP = 16
N_TENSOR = 4


def draw_norm_gain(key, part):
    key = jax.random.fold_in(key, 7)
    low_end = math.log(0.5)
    high_end = math.log(2.0)
    return jnp.exp(jax.random.uniform(key, (D,), jnp.float32, low_end, high_end))


def shard_levels(rng, dims, split, low, top_value):
    def one(dim, shards_of):
        draws = jax.random.uniform(jax.random.fold_in(jax.random.fold_in(rng, 6), dim), (shards_of,), jnp.float32, low / len(split), top_value / len(split))
        return jnp.repeat(jnp.exp(draws), dims[dim] // shards_of).reshape((-1,) + (1,) * (len(dims) - dim - 1))

    gain = one(*split[0])
    for cut in split[1:]:
        gain = gain * one(*cut)
    return gain


def scatter_about(own_key, dims, spread, bound, shards=(), kind=jnp.bfloat16):
    entries = jax.random.normal(own_key, dims, jnp.float32) * spread
    if len(shards) > 0:
        entries = shard_levels(own_key, dims, shards, -0.22, 0.18) * entries
    return jnp.clip(entries, min=-bound, max=bound).astype(kind)


def setup_inputs(seed: int = 0) -> dict:
    splits = jax.random.split(jax.random.key(seed), 11)
    hidden = scatter_about(splits[0], (N_REPLICA, TOKENS, D), 1.0, 6.0, ((0, 4), (1, 64)))
    norm_gain = draw_norm_gain(jax.random.fold_in(splits[10], 71), 0)
    attn_weight = scatter_about(splits[2], (N_REPLICA, D, HK, PACK), D ** -0.5, 0.09375, ((0, 4), (1, 16), (2, 4)))
    adam_first = scatter_about(splits[3], (N_REPLICA, D, HK, PACK), 1.0, 6.0, ((0, 4), (1, 16), (2, 4)), jnp.float32)
    adam_second = jnp.clip(jnp.exp(math.log(100.0) - 4.6051702 * jax.random.uniform(splits[4], (N_REPLICA, D, HK, PACK), jnp.float32) ** shard_levels(splits[4], (N_REPLICA, D, HK, PACK), ((0, 4), (1, 16), (2, 4)), -0.2, 0.2)), 1.0, 100.0)
    cotangent = scatter_about(splits[5], (N_REPLICA, TOKENS, D), 1.0, 6.0, ((0, 4), (1, 64)))
    pseudo_grad = scatter_about(splits[6], (N_REPLICA, FRAG), 1.0, 6.0, ((0, 4), (1, 64)))
    outer_params = scatter_about(splits[7], (FRAG,), 1.0, 6.0, ((0, 64),), jnp.float32)
    outer_moment = scatter_about(splits[8], (FRAG,), 0.5, 3.0, ((0, 64),), jnp.float32)
    inner_frag = scatter_about(splits[9], (N_REPLICA, FRAG), 1.0, 6.0, ((0, 4), (1, 64)))
    return {"hidden": hidden, "norm_gain": norm_gain, "attn_weight": attn_weight, "adam_first": adam_first, "adam_second": adam_second, "cotangent": cotangent, "pseudo_grad": pseudo_grad, "outer_params": outer_params, "outer_moment": outer_moment, "inner_frag": inner_frag}


ROPE_BASE = 500000.0
NORM_EPS = 1e-05
LEARN_RATE = 0.001
BETA_ONE = 0.9
BETA_TWO = 0.95
ADAM_EPS = 1e-08
DECAY = 0.1
CORRECT_ONE = 0.9999734386011124
CORRECT_TWO = 0.994079470779666
OUTER_RATE = 0.7
OUTER_MOMENTUM = 0.9
MIXING = 0.5

def rope_tables(length):
    positions = jnp.arange(length, dtype=jnp.float32)
    freqs = ROPE_BASE ** (-2.0 * jnp.arange(HD // 2, dtype=jnp.float32) / HD)
    angles = positions[:, None] * freqs[None, :]
    return (jnp.cos(angles), jnp.sin(angles))

def rotate(values, cosine, sine, direction):
    middle = values.shape[-1] // 2
    leading = values[..., :middle]
    trailing = values[..., middle:]
    return jnp.concatenate([leading * cosine - direction * trailing * sine, trailing * cosine + direction * leading * sine], axis=-1)

def probabilities(queries, keys_rot):
    scores = jnp.einsum('ntkgd,nskd->nkgts', queries.astype(jnp.float32), keys_rot.astype(jnp.float32)) * (1.0 / math.sqrt(HD))
    length = queries.shape[1]
    causal = jnp.arange(length)[:, None] >= jnp.arange(length)[None, :]
    scores = jnp.where(causal, scores, -jnp.inf)
    highest = lax.optimization_barrier(jnp.max(scores, axis=-1, keepdims=True))
    exponent = jnp.exp(scores - highest)
    return exponent / lax.optimization_barrier(jnp.sum(exponent, axis=-1, keepdims=True))

def set_sums(left, right):
    width = HK // N_TENSOR
    total = jnp.zeros((left.shape[0], right.shape[0]), jnp.float32)
    for index in range(N_TENSOR):
        term = jnp.einsum('tkc,dkc->td', left[:, index * width:(index + 1) * width], right[:, index * width:(index + 1) * width])
        term = lax.optimization_barrier(term.astype(jnp.bfloat16))
        total = total + term.astype(jnp.float32)
    return total

def adam_update(weight, first_moment, second_moment, gradient):
    first_new = BETA_ONE * first_moment + (1.0 - BETA_ONE) * gradient
    second_new = BETA_TWO * second_moment + (1.0 - BETA_TWO) * gradient * gradient
    weight_wide = weight.astype(jnp.float32)
    update = first_new / CORRECT_ONE / (jnp.sqrt(second_new / CORRECT_TWO) + ADAM_EPS) + DECAY * weight_wide
    return ((weight_wide - LEARN_RATE * update).astype(jnp.bfloat16), first_new, second_new)

def replica_step(hidden, norm_gain, weight, first_moment, second_moment, cotangent):
    group_size = HQ // HK
    qkv_width = (group_size + 2) * HD
    inputs = hidden.astype(jnp.float32)
    inverse_rms = lax.rsqrt(lax.optimization_barrier(jnp.mean(inputs * inputs, axis=-1, keepdims=True)) + NORM_EPS)
    normed = (inputs * inverse_rms * norm_gain).astype(jnp.bfloat16)
    qkv_weight = weight[:, :, :qkv_width].astype(jnp.float32)
    out_weight = weight[:, :, qkv_width:].astype(jnp.float32)
    projected = jnp.einsum('td,dkp->tkp', normed.astype(jnp.float32), qkv_weight)
    projected = projected.reshape(N_FSDP, TOK_DEV, HK, qkv_width)
    cosine, sine = rope_tables(TOK_DEV)
    q_cos = cosine[None, :, None, None, :]
    q_sin = sine[None, :, None, None, :]
    k_cos = cosine[None, :, None, :]
    k_sin = sine[None, :, None, :]
    queries = rotate(projected[..., :group_size * HD].reshape(N_FSDP, TOK_DEV, HK, group_size, HD), q_cos, q_sin, 1.0).astype(jnp.bfloat16)
    keys_rot = rotate(projected[..., group_size * HD:(group_size + 1) * HD], k_cos, k_sin, 1.0).astype(jnp.bfloat16)
    value_heads = projected[..., (group_size + 1) * HD:].astype(jnp.bfloat16)
    soft = probabilities(queries, keys_rot)
    soft_half = soft.astype(jnp.bfloat16)
    context = jnp.einsum('nkgts,nskd->ntkgd', soft_half.astype(jnp.float32), value_heads.astype(jnp.float32)).astype(jnp.bfloat16)
    context_flat = context.reshape(N_FSDP * TOK_DEV, HK, group_size * HD)
    attended = set_sums(context_flat.astype(jnp.float32), out_weight)
    layer_out = (inputs + attended).astype(jnp.bfloat16)
    upstream = cotangent.astype(jnp.float32)
    d_context = jnp.einsum('td,dkc->tkc', upstream, out_weight).astype(jnp.bfloat16)
    d_heads = d_context.reshape(N_FSDP, TOK_DEV, HK, group_size, HD).astype(jnp.float32)
    d_soft = jnp.einsum('ntkgd,nskd->nkgts', d_heads, value_heads.astype(jnp.float32))
    d_value = jnp.einsum('nkgts,ntkgd->nskd', soft_half.astype(jnp.float32), d_heads).astype(jnp.bfloat16)
    d_scores = (soft * (d_soft - lax.optimization_barrier(jnp.sum(d_soft * soft, axis=-1, keepdims=True))) * (1.0 / math.sqrt(HD))).astype(jnp.bfloat16)
    d_query = jnp.einsum('nkgts,nskd->ntkgd', d_scores.astype(jnp.float32), keys_rot.astype(jnp.float32))
    d_key = jnp.einsum('nkgts,ntkgd->nskd', d_scores.astype(jnp.float32), queries.astype(jnp.float32))
    d_query = rotate(d_query, q_cos, q_sin, -1.0).astype(jnp.bfloat16)
    d_key = rotate(d_key, k_cos, k_sin, -1.0).astype(jnp.bfloat16)
    d_projected = jnp.concatenate([d_query.reshape(N_FSDP, TOK_DEV, HK, group_size * HD), d_key, d_value], axis=-1)
    d_projected = d_projected.reshape(N_FSDP * TOK_DEV, HK, qkv_width)
    d_normed = set_sums(d_projected.astype(jnp.float32), qkv_weight)
    scaled = d_normed * norm_gain
    d_inputs = inverse_rms * scaled - inputs * inverse_rms ** 3 * lax.optimization_barrier(jnp.mean(inputs * scaled, axis=-1, keepdims=True))
    hidden_grad = (upstream + d_inputs).astype(jnp.bfloat16)

    def accumulate(totals, pieces):
        normed_seq, d_proj_seq, upstream_seq, context_seq = pieces
        qkv_part = jnp.einsum('td,tkp->dkp', normed_seq.astype(jnp.float32), d_proj_seq.astype(jnp.float32))
        out_part = jnp.einsum('td,tkc->dkc', upstream_seq.astype(jnp.float32), context_seq.astype(jnp.float32))
        term = jnp.concatenate([qkv_part, out_part], axis=-1).astype(jnp.bfloat16)
        term = lax.optimization_barrier(term)
        return (totals + term.astype(jnp.float32), None)
    pieces = (normed.reshape(N_FSDP, TOK_DEV, D), d_projected.reshape(N_FSDP, TOK_DEV, HK, qkv_width), cotangent.reshape(N_FSDP, TOK_DEV, D), context_flat.reshape(N_FSDP, TOK_DEV, HK, group_size * HD))
    gradient, _ = lax.scan(accumulate, jnp.zeros(weight.shape, jnp.float32), pieces)
    new_weight, new_first, new_second = adam_update(weight, first_moment, second_moment, gradient)
    return (layer_out, hidden_grad, new_weight, new_first, new_second)

def reference(hidden, norm_gain, attn_weight, adam_first, adam_second, cotangent, pseudo_grad, outer_params, outer_moment, inner_frag):
    results = [replica_step(hidden[replica_index], norm_gain, attn_weight[replica_index], adam_first[replica_index], adam_second[replica_index], cotangent[replica_index]) for replica_index in range(N_REPLICA)]
    stacked = [jnp.stack([item[slot] for item in results]) for slot in range(5)]
    mean_delta = lax.optimization_barrier(jnp.sum(pseudo_grad.astype(jnp.float32), axis=0)) / N_REPLICA
    new_moment = OUTER_MOMENTUM * outer_moment + mean_delta
    new_outer = outer_params - OUTER_RATE * (mean_delta + OUTER_MOMENTUM * new_moment)
    new_inner = (MIXING * inner_frag.astype(jnp.float32) + (1.0 - MIXING) * new_outer[None, :]).astype(jnp.bfloat16)
    return (stacked[0], stacked[1], stacked[2], stacked[3], stacked[4], new_outer, new_moment, new_inner)
```

```python
import math

import jax
import jax.numpy as jnp
from jax import lax
from jax.sharding import Mesh, PartitionSpec as P

HQ = 16
HK = 4
HD = 128
GROUP = HQ // HK
QKV = (GROUP + 2) * HD


ROPE_BASE = 500000.0
NORM_EPS = 1e-05
LEARN_RATE = 0.001
BETA_ONE = 0.9
BETA_TWO = 0.95
ADAM_EPS = 1e-08
DECAY = 0.1
CORRECT_ONE = 0.9999734386011124
CORRECT_TWO = 0.994079470779666
OUTER_RATE = 0.7
OUTER_MOMENTUM = 0.9
MIXING = 0.5

RING = 4


def rope_tables(length):
    positions = jnp.arange(length, dtype=jnp.float32)
    freqs = ROPE_BASE ** (-2.0 * jnp.arange(HD // 2, dtype=jnp.float32) / HD)
    angles = positions[:, None] * freqs[None, :]
    return (jnp.cos(angles), jnp.sin(angles))


def rotate(values, cosine, sine, direction):
    middle = values.shape[-1] // 2
    leading = values[..., :middle]
    trailing = values[..., middle:]
    return jnp.concatenate(
        [
            leading * cosine - direction * trailing * sine,
            trailing * cosine + direction * leading * sine,
        ],
        axis=-1,
    )


def shift(value, axis, step):
    size = lax.axis_size(axis)
    return lax.ppermute(value, axis, [(i, (i + step) % size) for i in range(size)])


def ring_gather(value, axis):
    half = value.shape[0] // 2
    before = shift(value, axis, 1)
    after = shift(value, axis, -1)
    across_top = shift(before[:half], axis, 1)
    across_bottom = shift(after[half:], axis, -1)
    return value, before, after, jnp.concatenate([across_top, across_bottom])


OFFSETS = (0, -1, 1, 2)


def gather_weight(value):
    rows = value.shape[0]
    x = lax.axis_index("x")
    z = lax.axis_index("zh")
    full = jnp.zeros((RING * RING * rows, value.shape[1]), value.dtype)
    for dz, block in zip(OFFSETS, ring_gather(value, "zh")):
        for dx, piece in zip(OFFSETS, ring_gather(block, "x")):
            start = (((x + dx) % RING) * RING + (z + dz) % RING) * rows
            full = lax.dynamic_update_slice(full, piece, (start, 0))
    return full


def add(left, right):
    return (left.astype(jnp.float32) + right.astype(jnp.float32)).astype(jnp.bfloat16)


def ring_reduce(blocks, axis):
    half = blocks[2].shape[0] // 2
    top = shift(blocks[2][:half], axis, 1)
    bottom = shift(blocks[2][half:], axis, -1)
    forward = jnp.concatenate([add(blocks[1][:half], top), blocks[1][half:]])
    backward = jnp.concatenate([blocks[3][:half], add(blocks[3][half:], bottom)])
    forward = shift(forward, axis, 1)
    backward = shift(backward, axis, -1)
    return (
        blocks[0].astype(jnp.float32) + forward.astype(jnp.float32) + backward.astype(jnp.float32)
    )


def reduce_weight(partial_value):
    rows = partial_value.shape[0] // (RING * RING)
    x = lax.axis_index("x")
    z = lax.axis_index("zh")

    def block(dx, dz):
        start = (((x + dx) % RING) * RING + (z + dz) % RING) * rows
        return lax.dynamic_slice_in_dim(partial_value, start, rows, 0)

    sums = {}
    for dz in (2, 1, 3, 0):
        total = ring_reduce([block(dx, dz) for dx in range(RING)], "x")
        sums[dz] = total.astype(jnp.bfloat16)
    return ring_reduce(sums, "zh")


def gather_rows(block):
    rows = block.shape[0]
    zl = lax.axis_index("zl")
    core = lax.axis_index("core")
    other = shift(block, "zl", 1)
    full = jnp.zeros((4 * rows, block.shape[1]), block.dtype)
    pieces = (
        (block, zl, core),
        (shift(block, "core", 1), zl, 1 - core),
        (other, 1 - zl, core),
        (shift(other, "core", 1), 1 - zl, 1 - core),
    )
    for piece, its_zl, its_core in pieces:
        full = lax.dynamic_update_slice(full, piece, ((its_zl * 2 + its_core) * rows, 0))
    return full


def reduce_rows(partial_value):
    rows = partial_value.shape[0] // 4
    zl = lax.axis_index("zl")
    core = lax.axis_index("core")

    def block(its_zl, its_core):
        return lax.dynamic_slice_in_dim(partial_value, (its_zl * 2 + its_core) * rows, rows, 0)

    away = add(block(1 - zl, core), shift(block(1 - zl, 1 - core), "core", 1))
    away = shift(away, "zl", 1)
    own = shift(block(zl, 1 - core), "core", 1).astype(jnp.float32)
    return own + block(zl, core).astype(jnp.float32) + away.astype(jnp.float32)


def probabilities(queries, keys_rot):
    scores = jnp.einsum("tgd,sd->gts", queries, keys_rot, preferred_element_type=jnp.float32) * (
        1.0 / math.sqrt(HD)
    )
    length = queries.shape[0]
    causal = jnp.arange(length)[:, None] >= jnp.arange(length)[None, :]
    scores = jnp.where(causal, scores, -jnp.inf)
    highest = jnp.max(scores, axis=-1, keepdims=True)
    exponent = jnp.exp(scores - highest)
    return exponent / jnp.sum(exponent, axis=-1, keepdims=True)


def dot(left, right, dims):
    return lax.dot_general(left, right, (dims, ((), ())), preferred_element_type=jnp.float32)


def per_device(
    hidden,
    norm_gain,
    attn_weight,
    adam_first,
    adam_second,
    cotangent,
    pseudo_grad,
    outer_params,
    outer_moment,
    inner_frag,
):
    own_weight = attn_weight[0, :, 0, :]
    qkv_weight = gather_weight(own_weight[:, :QKV])
    out_weight = lax.all_gather(own_weight[:, QKV:], ("x", "zh"), axis=0, tiled=True)
    inputs = hidden[0].astype(jnp.float32)
    inverse_rms = lax.rsqrt(jnp.mean(inputs * inputs, axis=-1, keepdims=True) + NORM_EPS)
    normed = (inputs * inverse_rms * norm_gain).astype(jnp.bfloat16)
    full_normed = gather_rows(normed)
    full_cotangent = gather_rows(cotangent[0])
    length = full_normed.shape[0]
    projected = dot(full_normed, qkv_weight, ((1,), (0,)))
    cosine, sine = rope_tables(length)
    q_cos = cosine[:, None, :]
    q_sin = sine[:, None, :]
    queries = rotate(
        projected[:, : GROUP * HD].reshape(length, GROUP, HD), q_cos, q_sin, 1.0
    ).astype(jnp.bfloat16)
    keys_rot = rotate(projected[:, GROUP * HD : (GROUP + 1) * HD], cosine, sine, 1.0).astype(
        jnp.bfloat16
    )
    value_heads = projected[:, (GROUP + 1) * HD :].astype(jnp.bfloat16)
    soft = probabilities(queries, keys_rot)
    soft_half = soft.astype(jnp.bfloat16)
    context = jnp.einsum(
        "gts,sd->tgd", soft_half, value_heads, preferred_element_type=jnp.float32
    ).astype(jnp.bfloat16)
    context_flat = context.reshape(length, GROUP * HD)
    out_part = dot(full_cotangent, context_flat, ((0,), (0,))).astype(jnp.bfloat16)
    out_gradient = lax.psum_scatter(
        out_part, ("x", "zh"), scatter_dimension=0, tiled=True
    ).astype(jnp.float32)
    attended = reduce_rows(dot(context_flat, out_weight, ((1,), (1,))).astype(jnp.bfloat16))
    layer_out = (inputs + attended).astype(jnp.bfloat16)
    d_context = dot(full_cotangent, out_weight, ((1,), (0,))).astype(jnp.bfloat16)
    d_heads = d_context.reshape(length, GROUP, HD)
    d_soft = jnp.einsum("tgd,sd->gts", d_heads, value_heads, preferred_element_type=jnp.float32)
    d_value = jnp.einsum(
        "gts,tgd->sd", soft_half, d_heads, preferred_element_type=jnp.float32
    ).astype(jnp.bfloat16)
    d_scores = (
        soft * (d_soft - jnp.sum(d_soft * soft, axis=-1, keepdims=True)) * (1.0 / math.sqrt(HD))
    ).astype(jnp.bfloat16)
    d_query = jnp.einsum("gts,sd->tgd", d_scores, keys_rot, preferred_element_type=jnp.float32)
    d_key = jnp.einsum("gts,tgd->sd", d_scores, queries, preferred_element_type=jnp.float32)
    d_query = rotate(d_query, q_cos, q_sin, -1.0).astype(jnp.bfloat16)
    d_key = rotate(d_key, cosine, sine, -1.0).astype(jnp.bfloat16)
    d_projected = jnp.concatenate(
        [d_query.reshape(length, GROUP * HD), d_key, d_value], axis=-1
    )
    qkv_part = dot(full_normed, d_projected, ((0,), (0,))).astype(jnp.bfloat16)
    qkv_gradient = reduce_weight(qkv_part)
    d_normed = reduce_rows(dot(d_projected, qkv_weight, ((1,), (1,))).astype(jnp.bfloat16))
    scaled = d_normed * norm_gain
    d_inputs = inverse_rms * scaled - inputs * inverse_rms**3 * jnp.mean(
        inputs * scaled, axis=-1, keepdims=True
    )
    hidden_grad = (cotangent[0].astype(jnp.float32) + d_inputs).astype(jnp.bfloat16)
    gradient = jnp.concatenate([qkv_gradient, out_gradient], axis=-1)[None, :, None, :]
    first_new = BETA_ONE * adam_first + (1.0 - BETA_ONE) * gradient
    second_new = BETA_TWO * adam_second + (1.0 - BETA_TWO) * gradient * gradient
    weight_wide = attn_weight.astype(jnp.float32)
    update = (
        first_new / CORRECT_ONE / (jnp.sqrt(second_new / CORRECT_TWO) + ADAM_EPS)
        + DECAY * weight_wide
    )
    new_weight = (weight_wide - LEARN_RATE * update).astype(jnp.bfloat16)
    replicas = lax.axis_size("replica")
    summed = lax.psum(pseudo_grad[0].astype(jnp.float32).astype(jnp.bfloat16), "replica").astype(
        jnp.float32
    )
    mean_delta = summed / replicas
    new_moment = OUTER_MOMENTUM * outer_moment + mean_delta
    new_outer = outer_params - OUTER_RATE * (mean_delta + OUTER_MOMENTUM * new_moment)
    new_inner = (MIXING * inner_frag[0].astype(jnp.float32) + (1.0 - MIXING) * new_outer).astype(
        jnp.bfloat16
    )
    return (
        layer_out[None],
        hidden_grad[None],
        new_weight,
        first_new,
        second_new,
        new_outer,
        new_moment,
        new_inner[None],
    )


def solution(mesh):
    fine = Mesh(mesh.devices.reshape(4, 4, 4, 2, 2), ("replica", "x", "zh", "zl", "core"))
    rows = ("x", "zh", "zl", "core")
    tokens = P("replica", rows, None)
    weights = P("replica", ("x", "zh"), ("zl", "core"), None)
    fragment = P("replica", rows)
    return jax.shard_map(
        per_device,
        mesh=fine,
        in_specs=(
            tokens,
            P(),
            weights,
            weights,
            weights,
            tokens,
            fragment,
            P(rows),
            P(rows),
            fragment,
        ),
        out_specs=(
            tokens,
            tokens,
            weights,
            weights,
            weights,
            P(rows),
            P(rows),
            fragment,
        ),
        check_vma=False,
    )
```

```python
import functools
import math

import jax
import jax.numpy as jnp
from jax import lax
from jax.experimental import pallas as pl
from jax.experimental.pallas import tpu as pltpu
from jax.sharding import Mesh, PartitionSpec as P

HQ = 16
HK = 4
HD = 128
GROUP = HQ // HK
QKV = (GROUP + 2) * HD


ROPE_BASE = 500000.0
NORM_EPS = 1e-05
LEARN_RATE = 0.001
BETA_ONE = 0.9
BETA_TWO = 0.95
ADAM_EPS = 1e-08
DECAY = 0.1
CORRECT_ONE = 0.9999734386011124
CORRECT_TWO = 0.994079470779666
OUTER_RATE = 0.7
OUTER_MOMENTUM = 0.9
MIXING = 0.5

RING = 4


def rope_tables(length):
    positions = jnp.arange(length, dtype=jnp.float32)
    freqs = ROPE_BASE ** (-2.0 * jnp.arange(HD // 2, dtype=jnp.float32) / HD)
    angles = positions[:, None] * freqs[None, :]
    cosine, sine = jnp.cos(angles), jnp.sin(angles)
    return (
        jnp.concatenate([cosine, cosine], axis=-1),
        jnp.concatenate([-sine, sine], axis=-1),
    )


TILE = 256
SCALE = 1.0 / math.sqrt(HD)


def swap_turn(values, cosine, sine):
    return values * cosine + pltpu.roll(values, HD // 2, 1) * sine


def mm(left, right, dims):
    return lax.dot_general(left, right, (dims, ((), ())), preferred_element_type=jnp.float32)


def tile_probabilities(queries, keys, place):
    scores = mm(queries, keys, ((1,), (1,))) * SCALE
    rows = lax.broadcasted_iota(jnp.int32, scores.shape, 0) + place * TILE
    columns = lax.broadcasted_iota(jnp.int32, scores.shape, 1)
    scores = jnp.where(rows >= columns, scores, -jnp.inf)
    exponent = jnp.exp(scores - jnp.max(scores, axis=-1, keepdims=True))
    return exponent / jnp.sum(exponent, axis=-1, keepdims=True)


def forward_kernel(projected, cosine, sine, rotated, context):
    cos = cosine[...]
    sin = sine[...]
    for head in range(GROUP + 1):
        part = pl.ds(head * HD, HD)
        rotated[:, part] = swap_turn(projected[:, part], cos, sin).astype(jnp.bfloat16)
    part = pl.ds((GROUP + 1) * HD, HD)
    rotated[:, part] = projected[:, part].astype(jnp.bfloat16)
    for place in range(projected.shape[0] // TILE):
        rows = pl.ds(place * TILE, TILE)
        known = pl.ds(0, (place + 1) * TILE)
        keys = rotated[known, pl.ds(GROUP * HD, HD)]
        values = rotated[known, pl.ds((GROUP + 1) * HD, HD)]
        for head in range(GROUP):
            part = pl.ds(head * HD, HD)
            probs = tile_probabilities(rotated[rows, part], keys, place).astype(jnp.bfloat16)
            context[rows, part] = mm(probs, values, ((1,), (0,))).astype(jnp.bfloat16)


def backward_kernel(rotated, d_context, cosine, sine, d_projected, d_keys, d_values):
    d_keys[...] = jnp.zeros_like(d_keys)
    d_values[...] = jnp.zeros_like(d_values)
    for place in range(rotated.shape[0] // TILE):
        rows = pl.ds(place * TILE, TILE)
        known = pl.ds(0, (place + 1) * TILE)
        keys = rotated[known, pl.ds(GROUP * HD, HD)]
        values = rotated[known, pl.ds((GROUP + 1) * HD, HD)]
        cos = cosine[rows, :]
        sin = sine[rows, :]
        for head in range(GROUP):
            part = pl.ds(head * HD, HD)
            queries = rotated[rows, part]
            upstream = d_context[rows, part]
            probs = tile_probabilities(queries, keys, place)
            d_probs = mm(upstream, values, ((1,), (1,)))
            d_values[known, :] += mm(probs.astype(jnp.bfloat16), upstream, ((0,), (0,)))
            d_scores = probs * (d_probs - jnp.sum(d_probs * probs, axis=-1, keepdims=True))
            d_scores = (d_scores * SCALE).astype(jnp.bfloat16)
            d_keys[known, :] += mm(d_scores, queries, ((0,), (0,)))
            d_queries = mm(d_scores, keys, ((1,), (0,)))
            d_projected[rows, part] = swap_turn(d_queries, cos, -sin).astype(jnp.bfloat16)
    d_projected[:, pl.ds(GROUP * HD, HD)] = swap_turn(
        d_keys[...], cosine[...], -sine[...]
    ).astype(jnp.bfloat16)
    d_projected[:, pl.ds((GROUP + 1) * HD, HD)] = d_values[...].astype(jnp.bfloat16)


def attention_forward(projected, cosine, sine):
    length = projected.shape[0]
    return pl.pallas_call(
        forward_kernel,
        out_shape=(
            jax.ShapeDtypeStruct((length, QKV), jnp.bfloat16),
            jax.ShapeDtypeStruct((length, GROUP * HD), jnp.bfloat16),
        ),
        cost_estimate=pl.CostEstimate(
            flops=4 * GROUP * length * length * HD, bytes_accessed=6 << 20, transcendentals=1 << 20
        ),
        compiler_params=pltpu.CompilerParams(vmem_limit_bytes=16 << 20),
        name="attention_forward",
    )(projected, cosine, sine)


def attention_backward(rotated, d_context, cosine, sine):
    length = rotated.shape[0]
    return pl.pallas_call(
        backward_kernel,
        out_shape=jax.ShapeDtypeStruct((length, QKV), jnp.bfloat16),
        scratch_shapes=[
            pltpu.VMEM((length, HD), jnp.float32),
            pltpu.VMEM((length, HD), jnp.float32),
        ],
        cost_estimate=LIGHT,
        compiler_params=pltpu.CompilerParams(vmem_limit_bytes=16 << 20),
        name="attention_backward",
    )(rotated, d_context, cosine, sine)


ADAM_ROWS = 64


def adam_kernel(n_qkv, starts, qkv_block, out_block, *refs):
    weight, first, second, new_weight, new_first, new_second = refs[-6:]
    qkv_came = (qkv_block,) + refs[:n_qkv]
    out_came = (out_block,) + refs[n_qkv:-6]
    blocks = weight.shape[1] // 128
    for place in range(blocks):
        part = pl.ds(place * 128, 128)
        if place < QKV // 128:
            terms = [ref[:, part].astype(jnp.float32) for ref in qkv_came]
        else:
            out_columns = pl.ds(place * 128 - QKV, 128)
            terms = [ref[:, out_columns].astype(jnp.float32) for ref in out_came]
        gradient = sum(terms[1:], terms[0])
        rows = pl.ds(place, weight.shape[0], stride=blocks)
        first_new = BETA_ONE * first[rows, :] + (1.0 - BETA_ONE) * gradient
        second_new = BETA_TWO * second[rows, :] + (1.0 - BETA_TWO) * gradient * gradient
        weight_wide = weight[:, part].astype(jnp.float32)
        update = (
            first_new / CORRECT_ONE / (jnp.sqrt(second_new / CORRECT_TWO) + ADAM_EPS)
            + DECAY * weight_wide
        )
        new_weight[:, part] = (weight_wide - LEARN_RATE * update).astype(jnp.bfloat16)
        new_first[rows, :] = first_new
        new_second[rows, :] = second_new


def adam_step(starts, qkv_part, out_own, qkv_came, out_came, weight, first, second):
    rows, columns = weight.shape
    blocks = columns // 128
    steps = rows // ADAM_ROWS

    def spec(shape):
        return pl.BlockSpec(shape, lambda i, starts: (i, 0))

    block = spec((ADAM_ROWS, columns))
    moment = spec((ADAM_ROWS * blocks, 128))
    moments = jax.ShapeDtypeStruct((rows * blocks, 128), jnp.float32)
    qkv_spec = spec((ADAM_ROWS, QKV))
    out_spec = spec((ADAM_ROWS, columns - QKV))
    own_spec = pl.BlockSpec((ADAM_ROWS, QKV), lambda i, starts: (starts[0] // ADAM_ROWS + i, 0))
    return pl.pallas_call(
        functools.partial(adam_kernel, len(qkv_came)),
        grid_spec=pltpu.PrefetchScalarGridSpec(
            num_scalar_prefetch=1,
            grid=(steps,),
            in_specs=[own_spec, out_spec]
            + [qkv_spec] * len(qkv_came)
            + [out_spec] * len(out_came)
            + [block, moment, moment],
        out_specs=(block, moment, moment),
        ),
        out_shape=(jax.ShapeDtypeStruct((rows, columns), jnp.bfloat16), moments, moments),
        cost_estimate=pl.CostEstimate(
            flops=20 * rows * columns, bytes_accessed=32 * rows * columns, transcendentals=0
        ),
        compiler_params=pltpu.CompilerParams(vmem_limit_bytes=24 << 20),
        name="adam",
    )(starts, qkv_part, out_own, *qkv_came, *out_came, weight, first, second)


SMEM = pl.BlockSpec(memory_space=pltpu.SMEM)
VMEM = pl.BlockSpec(memory_space=pltpu.VMEM)
LIGHT = pl.CostEstimate(flops=0, bytes_accessed=0, transcendentals=0)


def call_rows(name, kernel, starts, operands, shapes):
    held = 4 * sum(rows * columns for rows, columns in shapes)
    return pl.pallas_call(
        kernel,
        in_specs=[SMEM] + [VMEM] * len(operands),
        out_shape=[jax.ShapeDtypeStruct(shape, jnp.bfloat16) for shape in shapes],
        cost_estimate=LIGHT,
        compiler_params=pltpu.CompilerParams(vmem_limit_bytes=(4 << 20) + held),
        name=name,
    )(starts, *operands)


def move(name, starts, sources, shapes, copies):
    def kernel(starts, *refs):
        for source, from_row, rows, target, to_row in copies:
            if isinstance(to_row, list):
                to_row = pl.multiple_of(starts[to_row[0]], 128)
            target = refs[len(sources) + target]
            target[pl.ds(to_row, rows), :] = refs[source][pl.ds(from_row, rows), :]

    return call_rows(name, kernel, starts, sources, shapes)


def combine(name, starts, part, came, outputs):
    columns = part.shape[1]

    def kernel(starts, part, *refs):
        for target, segs in zip(refs[len(came) :], outputs):
            to_row = 0
            for rows, block, offset, terms in segs:
                first = pl.multiple_of(starts[block] + offset, 128)
                total = part[pl.ds(first, rows), :]
                if terms:
                    total = total.astype(jnp.float32)
                    for array, row in terms:
                        total = total + refs[array][pl.ds(row, rows), :].astype(jnp.float32)
                target[pl.ds(to_row, rows), :] = total.astype(jnp.bfloat16)
                to_row += rows

    shapes = [(sum(seg[0] for seg in segs), columns) for segs in outputs]
    return call_rows(name, kernel, starts, [part, *came], shapes)


BLOCK = 512


def weight_gradient_kernel(tokens, upstream, gradient):
    gradient[...] = mm(tokens[...], upstream[...], ((0,), (0,))).astype(jnp.bfloat16)


def weight_gradient(tokens, upstream):
    length, model = tokens.shape
    columns = upstream.shape[1]
    return pl.pallas_call(
        weight_gradient_kernel,
        grid=(model // BLOCK,),
        in_specs=[
            pl.BlockSpec((length, BLOCK), lambda i: (0, i)),
            pl.BlockSpec((length, columns), lambda i: (0, 0)),
        ],
        out_specs=pl.BlockSpec((BLOCK, columns), lambda i: (i, 0)),
        out_shape=jax.ShapeDtypeStruct((model, columns), jnp.bfloat16),
        cost_estimate=LIGHT,
        compiler_params=pltpu.CompilerParams(vmem_limit_bytes=16 << 20),
        name="weight_gradient",
    )(tokens, upstream)


def input_gradient_kernel(upstream, weight, gradient):
    gradient[...] = mm(upstream[...], weight[...], ((1,), (1,))).astype(jnp.bfloat16)


def input_gradient(upstream, weight):
    length, columns = upstream.shape
    model = weight.shape[0]
    return pl.pallas_call(
        input_gradient_kernel,
        grid=(model // BLOCK,),
        in_specs=[
            pl.BlockSpec((length, columns), lambda i: (0, 0)),
            pl.BlockSpec((BLOCK, columns), lambda i: (i, 0)),
        ],
        out_specs=pl.BlockSpec((length, BLOCK), lambda i: (0, i)),
        out_shape=jax.ShapeDtypeStruct((length, model), jnp.bfloat16),
        cost_estimate=LIGHT,
        compiler_params=pltpu.CompilerParams(vmem_limit_bytes=16 << 20),
        name="input_gradient",
    )(upstream, weight)


def shift(value, axis, step):
    size = lax.axis_size(axis)
    return lax.ppermute(value, axis, [(i, (i + step) % size) for i in range(size)])


def barrier(*values):
    return lax.optimization_barrier(values)


def add(left, right):
    return (left.astype(jnp.float32) + right.astype(jnp.float32)).astype(jnp.bfloat16)


def sum_three(left, middle, right):
    return left.astype(jnp.float32) + middle.astype(jnp.float32) + right.astype(jnp.float32)


def place_rows(pieces, rows):
    full = jnp.zeros((len(pieces) * rows, pieces[0][0].shape[1]), pieces[0][0].dtype)
    for piece, index in pieces:
        full = lax.dynamic_update_slice(full, piece, (index * rows, 0))
    return full


def first_rows(rows):
    x = lax.axis_index("x")
    z = lax.axis_index("zh")
    return jnp.stack(
        [
            ((((x + dx) % RING) * RING + (z + dz) % RING) * rows + offset).astype(jnp.int32)
            for offset in (0, rows // 2)
            for dx in range(RING)
            for dz in range(RING)
        ]
    )


def at(dx, dz):
    return [(dx % RING) * RING + dz % RING]


def low(dx, dz):
    return [at(dx, dz)[0] + RING * RING]


def first_tokens(rows):
    zl = lax.axis_index("zl")
    core = lax.axis_index("core")
    return jnp.stack(
        [
            ((its_zl * 2 + its_core) * rows).astype(jnp.int32)
            for its_zl, its_core in ((zl, core), (zl, 1 - core), (1 - zl, core), (1 - zl, 1 - core))
        ]
    )


def place_tokens(name, starts, *pieces):
    rows, columns = pieces[0].shape
    copies = [(piece, 0, rows, 0, [piece]) for piece in range(4)]
    return move(name, starts, pieces, [(4 * rows, columns)], copies)[0]


def gather_all(starts, token_starts, weight, normed, cotangent, beside):
    rows, columns = weight.shape
    half = rows // 2

    z_before = shift(weight, "zh", 1)
    z_after = shift(weight, "zh", -1)
    x_before = shift(weight, "x", 1)
    x_after = shift(weight, "x", -1)
    x_across = shift(weight, "x", 2)
    z_before, z_after, x_before, x_after, x_across, normed, starts, token_starts = barrier(
        z_before, z_after, x_before, x_after, x_across, normed, starts, token_starts
    )

    sides, z_on, z_back = move(
        "pack_sides",
        starts,
        [z_before, z_after],
        [(2 * rows, columns), (half, columns), (half, columns)],
        [
            (0, 0, half, 1, 0),
            (1, half, half, 2, 0),
            (0, 0, rows, 0, 0),
            (1, 0, rows, 0, rows),
        ],
    )
    from_before = shift(sides, "x", 1)
    from_after = shift(sides, "x", -1)
    z_top = shift(z_on, "zh", 1)
    z_bottom = shift(z_back, "zh", -1)
    normed_core = shift(normed, "core", 1)
    z_top, z_bottom, from_before, from_after, normed, normed_core = barrier(
        z_top, z_bottom, from_before, from_after, normed, normed_core
    )

    to_after, to_before = move(
        "pack_across",
        starts,
        [z_top, z_bottom, from_before, from_after],
        [(2 * rows, columns)] * 2,
        [
            (0, 0, half, 0, 0),
            (1, 0, half, 0, half),
            (2, 0, rows, 0, rows),
            (0, 0, half, 1, 0),
            (1, 0, half, 1, half),
            (3, rows, rows, 1, rows),
        ],
    )
    more_before = shift(to_after, "x", 1)
    more_after = shift(to_before, "x", -1)
    normed_zl = shift(normed, "zl", 1)
    cotangent_core = shift(cotangent, "core", 1)
    more_before, more_after, normed_zl, cotangent, cotangent_core, *beside = barrier(
        more_before, more_after, normed_zl, cotangent, cotangent_core, *beside
    )

    last_on, last_back = move(
        "pack_last",
        starts,
        [more_before, more_after],
        [(half, columns)] * 2,
        [(0, 0, half, 0, 0), (1, half, half, 1, 0)],
    )
    last_top = shift(last_on, "x", 1)
    last_bottom = shift(last_back, "x", -1)
    normed_both = shift(normed_zl, "core", 1)
    cotangent_zl = shift(cotangent, "zl", 1)
    full_normed = place_tokens(
        "place_normed", token_starts, normed, normed_core, normed_zl, normed_both
    )
    last_top, last_bottom, full_normed = barrier(last_top, last_bottom, full_normed)

    (full,) = move(
        "place_weight",
        starts,
        [
            weight,
            z_before,
            z_after,
            x_before,
            x_after,
            x_across,
            from_before,
            from_after,
            z_top,
            z_bottom,
            more_before,
            more_after,
            last_top,
            last_bottom,
        ],
        [(RING * RING * rows, columns)],
        [
            (0, 0, rows, 0, at(0, 0)),
            (1, 0, rows, 0, at(0, -1)),
            (2, 0, rows, 0, at(0, 1)),
            (3, 0, rows, 0, at(-1, 0)),
            (4, 0, rows, 0, at(1, 0)),
            (5, 0, rows, 0, at(2, 0)),
            (6, 0, rows, 0, at(-1, -1)),
            (6, rows, rows, 0, at(-1, 1)),
            (7, 0, rows, 0, at(1, -1)),
            (7, rows, rows, 0, at(1, 1)),
            (8, 0, half, 0, at(0, 2)),
            (9, 0, half, 0, low(0, 2)),
            (10, 0, rows, 0, at(-1, 2)),
            (10, rows, rows, 0, at(2, -1)),
            (11, 0, rows, 0, at(1, 2)),
            (11, rows, rows, 0, at(2, 1)),
            (12, 0, half, 0, at(2, 2)),
            (13, 0, half, 0, low(2, 2)),
        ],
    )
    return full, full_normed, (token_starts, cotangent, cotangent_core, cotangent_zl), beside


def reduce_core(name, token_starts, part):
    rows = part.shape[0] // 4
    (leaving,) = combine(
        name + "_leave", token_starts, part, [], [[(rows, 3, 0, []), (rows, 1, 0, [])]]
    )
    return combine(
        name + "_add",
        token_starts,
        part,
        [shift(leaving, "core", 1)],
        [[(rows, 2, 0, [(0, 0)])], [(rows, 0, 0, [(0, rows)])]],
    )


def wide(value):
    return value.astype(jnp.float32)


def dot(left, right, dims):
    return lax.dot_general(left, right, (dims, ((), ())), preferred_element_type=jnp.float32)


def per_device(
    hidden,
    norm_gain,
    attn_weight,
    adam_first,
    adam_second,
    cotangent,
    pseudo_grad,
    outer_params,
    outer_moment,
    inner_frag,
):
    own_weight = attn_weight[0, :, 0, :]
    inputs = hidden[0].astype(jnp.float32)
    inverse_rms = lax.rsqrt(jnp.mean(inputs * inputs, axis=-1, keepdims=True) + NORM_EPS)
    normed = (inputs * inverse_rms * norm_gain).astype(jnp.bfloat16)
    summed = lax.psum(pseudo_grad[0].astype(jnp.float32).astype(jnp.bfloat16), "replica").astype(
        jnp.float32
    )
    mean_delta = summed / lax.axis_size("replica")
    new_moment = OUTER_MOMENTUM * outer_moment + mean_delta
    new_outer = outer_params - OUTER_RATE * (mean_delta + OUTER_MOMENTUM * new_moment)
    new_inner = (MIXING * inner_frag[0].astype(jnp.float32) + (1.0 - MIXING) * new_outer).astype(
        jnp.bfloat16
    )
    cosine, sine = rope_tables(4 * normed.shape[0])
    starts = first_rows(own_weight.shape[0])
    full_weight, full_normed, cotangent_parts, beside = gather_all(
        starts,
        first_tokens(normed.shape[0]),
        own_weight,
        normed,
        cotangent[0],
        (new_moment, new_outer, new_inner[None], cosine, sine),
    )
    new_moment, new_outer, new_inner, cosine, sine = beside
    qkv_weight = full_weight[:, :QKV]
    out_weight = full_weight[:, QKV:]
    rows = own_weight.shape[0]
    half = rows // 2
    projected = dot(full_normed, qkv_weight, ((1,), (0,)))
    rotated, context = attention_forward(projected, cosine, sine)
    rows = own_weight.shape[0]
    half = rows // 2

    attended_part = dot(context, out_weight, ((1,), (1,))).astype(jnp.bfloat16)
    token_starts, own_cotangent, cotangent_core, cotangent_zl = cotangent_parts
    attended_part, cotangent_zl = barrier(attended_part, cotangent_zl)
    cotangent_both = shift(cotangent_zl, "core", 1)
    full_cotangent = place_tokens(
        "place_cotangent", token_starts, own_cotangent, cotangent_core, cotangent_zl, cotangent_both
    )
    out_part = dot(full_cotangent, context, ((0,), (0,))).astype(jnp.bfloat16)
    to_after, to_before = combine(
        "out_first",
        starts,
        out_part,
        [],
        [
            [(rows, 10, 0, []), (rows, 9, 0, [])],
            [(rows, 11, 0, []), (rows, 8, 0, [])],
        ],
    )
    out_forward = shift(to_after, "x", 1)
    out_backward = shift(to_before, "x", -1)
    attended_away, attended_own = reduce_core("attended", token_starts, attended_part)
    d_context = dot(full_cotangent, out_weight, ((1,), (0,))).astype(jnp.bfloat16)
    out_forward, out_backward, attended_away, d_context = barrier(
        out_forward, out_backward, attended_away, d_context
    )

    to_after, to_before = combine(
        "out_second",
        starts,
        out_part,
        [out_forward, out_backward],
        [
            [
                (rows, 6, 0, [(0, 0)]),
                (rows, 5, 0, [(0, rows)]),
                (rows, 7, 0, []),
                (rows, 4, 0, []),
            ],
            [
                (rows, 14, 0, []),
                (rows, 13, 0, []),
                (rows, 15, 0, [(1, 0)]),
                (rows, 12, 0, [(1, rows)]),
            ],
        ],
    )
    to_after, to_before, d_context = barrier(to_after, to_before, d_context)
    out_before = shift(to_after, "x", 1)
    out_after = shift(to_before, "x", -1)
    attended_away = shift(attended_away, "zl", 1)
    d_projected = attention_backward(rotated, d_context, cosine, sine)
    d_partial = input_gradient(d_projected, full_weight)
    d_away, d_own = reduce_core("d_normed", token_starts, d_partial)
    d_away, d_own, d_projected = barrier(d_away, d_own, d_projected)
    qkv_part = weight_gradient(full_normed, d_projected)
    to_after, to_before = combine(
        "qkv_first",
        starts,
        qkv_part,
        [],
        [
            [(rows, 10, 0, []), (half, 9, 0, [])],
            [(half, 9, half, []), (rows, 11, 0, [])],
        ],
    )
    out_before, out_after, attended_away, to_after, to_before, d_away = barrier(
        out_before, out_after, attended_away, to_after, to_before, d_away
    )
    forward = shift(to_after, "x", 1)
    backward = shift(to_before, "x", -1)
    d_away = shift(d_away, "zl", 1)
    out_top, out_bottom = combine(
        "out_third",
        starts,
        out_part,
        [out_before, out_after],
        [
            [(half, 2, 0, [(0, 0), (1, 0)])],
            [(half, 2, half, [(0, half), (1, half)])],
        ],
    )
    out_top = shift(out_top, "zh", 1)
    out_bottom = shift(out_bottom, "zh", -1)
    layer_out = sum_three(hidden[0], attended_own, attended_away).astype(jnp.bfloat16)
    forward, backward, out_top, out_bottom, d_away, layer_out = barrier(
        forward, backward, out_top, out_bottom, d_away, layer_out
    )

    to_after, to_before = combine(
        "qkv_second",
        starts,
        qkv_part,
        [forward],
        [[(rows, 6, 0, [(0, 0)])], [(rows, 14, 0, [])]],
    )
    across_before = shift(to_after, "x", 1)
    across_after = shift(to_before, "x", -1)
    out_on, out_back, out_own = combine(
        "out_fourth",
        starts,
        out_part,
        [out_before, out_after, out_top, out_bottom],
        [
            [
                (half, 1, 0, [(0, rows), (1, rows), (2, 0)]),
                (half, 1, half, [(0, rows + half), (1, rows + half)]),
            ],
            [
                (half, 3, 0, [(0, 2 * rows), (1, 2 * rows)]),
                (half, 3, half, [(0, 2 * rows + half), (1, 2 * rows + half), (3, 0)]),
            ],
            [(rows, 0, 0, [(0, 3 * rows), (1, 3 * rows)])],
        ],
    )
    out_came = [shift(out_on, "zh", 1), shift(out_back, "zh", -1)]
    across_before, across_after, *out_came = barrier(across_before, across_after, *out_came)

    top, bottom, to_after, to_before = combine(
        "qkv_third",
        starts,
        qkv_part,
        [forward, backward, across_before, across_after],
        [
            [(half, 2, 0, [(2, 0), (3, 0)])],
            [(half, 2, half, [(2, half), (3, half)])],
            [(half, 5, 0, [(0, rows)]), (half, 5, half, []), (rows, 7, 0, [])],
            [(half, 13, 0, []), (half, 13, half, [(1, 0)]), (rows, 15, 0, [(1, half)])],
        ],
    )
    sides_before = shift(to_after, "x", 1)
    sides_after = shift(to_before, "x", -1)
    top = shift(top, "zh", 1)
    bottom = shift(bottom, "zh", -1)
    x_on, x_back, x_two = combine(
        "qkv_own", starts, qkv_part, [], [[(rows, 4, 0, [])], [(rows, 12, 0, [])], [(rows, 8, 0, [])]]
    )
    top, bottom, sides_before, sides_after, x_on, x_back, x_two = barrier(
        top, bottom, sides_before, sides_after, x_on, x_back, x_two
    )

    z_on, z_back = combine(
        "qkv_fourth",
        starts,
        qkv_part,
        [sides_before, sides_after, top, bottom],
        [
            [
                (half, 1, 0, [(0, 0), (1, 0), (2, 0)]),
                (half, 1, half, [(0, half), (1, half)]),
            ],
            [
                (half, 3, 0, [(0, rows), (1, rows)]),
                (half, 3, half, [(0, rows + half), (1, rows + half), (3, 0)]),
            ],
        ],
    )
    qkv_came = [
        shift(z_on, "zh", 1),
        shift(z_back, "zh", -1),
        shift(x_on, "x", 1),
        shift(x_back, "x", -1),
        shift(x_two, "x", 2),
    ]
    d_normed = wide(d_own) + wide(d_away)
    scaled = d_normed * norm_gain
    d_inputs = inverse_rms * scaled - inputs * inverse_rms**3 * jnp.mean(
        inputs * scaled, axis=-1, keepdims=True
    )
    hidden_grad = (cotangent[0].astype(jnp.float32) + d_inputs).astype(jnp.bfloat16)
    flat = (-1, 128)
    new_weight, first_new, second_new = adam_step(
        starts,
        qkv_part,
        out_own,
        qkv_came,
        out_came,
        own_weight,
        adam_first.reshape(flat),
        adam_second.reshape(flat),
    )
    new_weight = new_weight.reshape(attn_weight.shape)
    first_new = first_new.reshape(adam_first.shape)
    second_new = second_new.reshape(adam_second.shape)
    return (
        layer_out[None],
        hidden_grad[None],
        new_weight,
        first_new,
        second_new,
        new_outer,
        new_moment,
        new_inner,
    )


def solution(mesh):
    fine = Mesh(mesh.devices.reshape(4, 4, 4, 2, 2), ("replica", "x", "zh", "zl", "core"))
    rows = ("x", "zh", "zl", "core")
    tokens = P("replica", rows, None)
    weights = P("replica", ("x", "zh"), ("zl", "core"), None)
    fragment = P("replica", rows)
    return jax.shard_map(
        per_device,
        mesh=fine,
        in_specs=(
            tokens,
            P(),
            weights,
            weights,
            weights,
            tokens,
            fragment,
            P(rows),
            P(rows),
            fragment,
        ),
        out_specs=(
            tokens,
            tokens,
            weights,
            weights,
            weights,
            P(rows),
            P(rows),
            fragment,
        ),
        check_vma=False,
    )
```

```python
import functools
import math

import jax
import jax.numpy as jnp
from jax import lax
from jax.experimental import pallas as pl
from jax.experimental.pallas import tpu as pltpu
from jax.sharding import Mesh, PartitionSpec as P

HQ = 16
HK = 4
HD = 128
GROUP = HQ // HK
QKV = (GROUP + 2) * HD


ROPE_BASE = 500000.0
NORM_EPS = 1e-05
LEARN_RATE = 0.001
BETA_ONE = 0.9
BETA_TWO = 0.95
ADAM_EPS = 1e-08
DECAY = 0.1
CORRECT_ONE = 0.9999734386011124
CORRECT_TWO = 0.994079470779666
OUTER_RATE = 0.7
OUTER_MOMENTUM = 0.9
MIXING = 0.5

RING = 4


def rope_tables(length):
    positions = jnp.arange(length, dtype=jnp.float32)
    freqs = ROPE_BASE ** (-2.0 * jnp.arange(HD // 2, dtype=jnp.float32) / HD)
    angles = positions[:, None] * freqs[None, :]
    cosine, sine = jnp.cos(angles), jnp.sin(angles)
    return (
        jnp.concatenate([cosine, cosine], axis=-1),
        jnp.concatenate([-sine, sine], axis=-1),
    )


TILE = 256
SCALE = 1.0 / math.sqrt(HD)


def swap_turn(values, cosine, sine):
    return values * cosine + pltpu.roll(values, HD // 2, 1) * sine


def mm(left, right, dims):
    return lax.dot_general(left, right, (dims, ((), ())), preferred_element_type=jnp.float32)


def tile_probabilities(queries, keys, place):
    scores = mm(queries, keys, ((1,), (1,))) * SCALE
    rows = lax.broadcasted_iota(jnp.int32, scores.shape, 0) + place * TILE
    columns = lax.broadcasted_iota(jnp.int32, scores.shape, 1)
    scores = jnp.where(rows >= columns, scores, -jnp.inf)
    exponent = jnp.exp(scores - jnp.max(scores, axis=-1, keepdims=True))
    return exponent / jnp.sum(exponent, axis=-1, keepdims=True)


def forward_kernel(projected, cosine, sine, rotated, context):
    cos = cosine[...]
    sin = sine[...]
    for head in range(GROUP + 1):
        part = pl.ds(head * HD, HD)
        rotated[:, part] = swap_turn(projected[:, part], cos, sin).astype(jnp.bfloat16)
    part = pl.ds((GROUP + 1) * HD, HD)
    rotated[:, part] = projected[:, part].astype(jnp.bfloat16)
    for place in range(projected.shape[0] // TILE):
        rows = pl.ds(place * TILE, TILE)
        known = pl.ds(0, (place + 1) * TILE)
        keys = rotated[known, pl.ds(GROUP * HD, HD)]
        values = rotated[known, pl.ds((GROUP + 1) * HD, HD)]
        for head in range(GROUP):
            part = pl.ds(head * HD, HD)
            probs = tile_probabilities(rotated[rows, part], keys, place).astype(jnp.bfloat16)
            context[rows, part] = mm(probs, values, ((1,), (0,))).astype(jnp.bfloat16)


def backward_kernel(rotated, d_context, cosine, sine, d_projected, d_keys, d_values):
    d_keys[...] = jnp.zeros_like(d_keys)
    d_values[...] = jnp.zeros_like(d_values)
    for place in range(rotated.shape[0] // TILE):
        rows = pl.ds(place * TILE, TILE)
        known = pl.ds(0, (place + 1) * TILE)
        keys = rotated[known, pl.ds(GROUP * HD, HD)]
        values = rotated[known, pl.ds((GROUP + 1) * HD, HD)]
        cos = cosine[rows, :]
        sin = sine[rows, :]
        for head in range(GROUP):
            part = pl.ds(head * HD, HD)
            queries = rotated[rows, part]
            upstream = d_context[rows, part]
            probs = tile_probabilities(queries, keys, place)
            d_probs = mm(upstream, values, ((1,), (1,)))
            d_values[known, :] += mm(probs.astype(jnp.bfloat16), upstream, ((0,), (0,)))
            d_scores = probs * (d_probs - jnp.sum(d_probs * probs, axis=-1, keepdims=True))
            d_scores = (d_scores * SCALE).astype(jnp.bfloat16)
            d_keys[known, :] += mm(d_scores, queries, ((0,), (0,)))
            d_queries = mm(d_scores, keys, ((1,), (0,)))
            d_projected[rows, part] = swap_turn(d_queries, cos, -sin).astype(jnp.bfloat16)
    d_projected[:, pl.ds(GROUP * HD, HD)] = swap_turn(
        d_keys[...], cosine[...], -sine[...]
    ).astype(jnp.bfloat16)
    d_projected[:, pl.ds((GROUP + 1) * HD, HD)] = d_values[...].astype(jnp.bfloat16)


def attention_forward(projected, cosine, sine):
    length = projected.shape[0]
    return pl.pallas_call(
        forward_kernel,
        out_shape=(
            jax.ShapeDtypeStruct((length, QKV), jnp.bfloat16),
            jax.ShapeDtypeStruct((length, GROUP * HD), jnp.bfloat16),
        ),
        cost_estimate=LIGHT,
        compiler_params=pltpu.CompilerParams(vmem_limit_bytes=16 << 20),
        name="attention_forward",
    )(projected, cosine, sine)


def attention_backward(rotated, d_context, cosine, sine):
    length = rotated.shape[0]
    return pl.pallas_call(
        backward_kernel,
        out_shape=jax.ShapeDtypeStruct((length, QKV), jnp.bfloat16),
        scratch_shapes=[
            pltpu.VMEM((length, HD), jnp.float32),
            pltpu.VMEM((length, HD), jnp.float32),
        ],
        cost_estimate=LIGHT,
        compiler_params=pltpu.CompilerParams(vmem_limit_bytes=16 << 20),
        name="attention_backward",
    )(rotated, d_context, cosine, sine)


ADAM_ROWS = 64


def adam_kernel(n_qkv, qkv_block, out_block, *refs):
    weight, first, second, new_weight, new_first, new_second = refs[-6:]
    qkv_came = (qkv_block,) + refs[:n_qkv]
    out_came = (out_block,) + refs[n_qkv:-6]
    blocks = weight.shape[1] // 128
    for place in range(blocks):
        part = pl.ds(place * 128, 128)
        if place < QKV // 128:
            terms = [ref[:, part].astype(jnp.float32) for ref in qkv_came]
        else:
            out_columns = pl.ds(place * 128 - QKV, 128)
            terms = [ref[:, out_columns].astype(jnp.float32) for ref in out_came]
        gradient = sum(terms[1:], terms[0])
        rows = pl.ds(place, weight.shape[0], stride=blocks)
        first_new = BETA_ONE * first[rows, :] + (1.0 - BETA_ONE) * gradient
        second_new = BETA_TWO * second[rows, :] + (1.0 - BETA_TWO) * gradient * gradient
        weight_wide = weight[:, part].astype(jnp.float32)
        update = (
            first_new / CORRECT_ONE / (jnp.sqrt(second_new / CORRECT_TWO) + ADAM_EPS)
            + DECAY * weight_wide
        )
        new_weight[:, part] = (weight_wide - LEARN_RATE * update).astype(jnp.bfloat16)
        new_first[rows, :] = first_new
        new_second[rows, :] = second_new


def adam_step(qkv_own, out_own, qkv_came, out_came, weight, first, second):
    rows, columns = weight.shape
    blocks = columns // 128
    steps = rows // ADAM_ROWS

    def spec(shape):
        return pl.BlockSpec(shape, lambda i: (i, 0))

    block = spec((ADAM_ROWS, columns))
    moment = spec((ADAM_ROWS * blocks, 128))
    moments = jax.ShapeDtypeStruct((rows * blocks, 128), jnp.float32)
    qkv_spec = spec((ADAM_ROWS, QKV))
    out_spec = spec((ADAM_ROWS, columns - QKV))
    return pl.pallas_call(
        functools.partial(adam_kernel, len(qkv_came)),
        grid=(steps,),
        in_specs=[qkv_spec, out_spec]
        + [qkv_spec] * len(qkv_came)
        + [out_spec] * len(out_came)
        + [block, moment, moment],
        out_specs=(block, moment, moment),
        out_shape=(jax.ShapeDtypeStruct((rows, columns), jnp.bfloat16), moments, moments),
        cost_estimate=pl.CostEstimate(
            flops=20 * rows * columns, bytes_accessed=32 * rows * columns, transcendentals=0
        ),
        compiler_params=pltpu.CompilerParams(vmem_limit_bytes=24 << 20),
        name="adam",
    )(qkv_own, out_own, *qkv_came, *out_came, weight, first, second)


SMEM = pl.BlockSpec(memory_space=pltpu.SMEM)
VMEM = pl.BlockSpec(memory_space=pltpu.VMEM)
LIGHT = pl.CostEstimate(flops=0, bytes_accessed=0, transcendentals=0)


def call_rows(name, kernel, starts, operands, shapes):
    held = 4 * sum(rows * columns for rows, columns in shapes)
    return pl.pallas_call(
        kernel,
        in_specs=[SMEM] + [VMEM] * len(operands),
        out_shape=[jax.ShapeDtypeStruct(shape, jnp.bfloat16) for shape in shapes],
        cost_estimate=LIGHT,
        compiler_params=pltpu.CompilerParams(vmem_limit_bytes=(4 << 20) + held),
        name=name,
    )(starts, *operands)


def move(name, starts, sources, shapes, copies):
    def kernel(starts, *refs):
        for source, from_row, rows, target, to_row in copies:
            if isinstance(to_row, list):
                place, offset = to_row
                to_row = pl.multiple_of(starts[place] + offset, math.gcd(128, offset))
            target = refs[len(sources) + target]
            target[pl.ds(to_row, rows), :] = refs[source][pl.ds(from_row, rows), :]

    return call_rows(name, kernel, starts, sources, shapes)


def combine(name, starts, part, came, outputs):
    columns = part.shape[1]

    def kernel(starts, part, *refs):
        for target, segs in zip(refs[len(came) :], outputs):
            to_row = 0
            for rows, block, offset, terms in segs:
                first = pl.multiple_of(starts[block] + offset, math.gcd(128, offset))
                total = part[pl.ds(first, rows), :]
                if terms:
                    total = total.astype(jnp.float32)
                    for array, row in terms:
                        total = total + refs[array][pl.ds(row, rows), :].astype(jnp.float32)
                target[pl.ds(to_row, rows), :] = total.astype(jnp.bfloat16)
                to_row += rows

    shapes = [(sum(seg[0] for seg in segs), columns) for segs in outputs]
    return call_rows(name, kernel, starts, [part, *came], shapes)


BLOCK = 512


def product(name, kernel, shape, *operands):
    return pl.pallas_call(
        kernel,
        in_specs=[VMEM] * len(operands),
        out_shape=jax.ShapeDtypeStruct(shape, jnp.bfloat16),
        cost_estimate=LIGHT,
        compiler_params=pltpu.CompilerParams(vmem_limit_bytes=24 << 20),
        name=name,
    )(*operands)


def weight_gradient(tokens, upstream):
    model = tokens.shape[1]

    def kernel(tokens, upstream, gradient):
        right = upstream[...]
        for first in range(0, model, BLOCK):
            part = pl.ds(first, BLOCK)
            block = mm(tokens[:, part], right, ((0,), (0,)))
            gradient[part, :] = block.astype(jnp.bfloat16)

    return product("weight_gradient", kernel, (model, upstream.shape[1]), tokens, upstream)


def through_weight(name, left, weight, column):
    length, columns = left.shape
    model = weight.shape[0]

    def kernel(left, weight, total):
        rows = left[...]
        for first in range(0, model, BLOCK):
            part = pl.ds(first, BLOCK)
            block = mm(rows, weight[part, pl.ds(column, columns)], ((1,), (1,)))
            total[:, part] = block.astype(jnp.bfloat16)

    return product(name, kernel, (length, model), left, weight)


def shift(value, axis, step):
    size = lax.axis_size(axis)
    return lax.ppermute(value, axis, [(i, (i + step) % size) for i in range(size)])


def barrier(*values):
    return lax.optimization_barrier(values)


def add(left, right):
    return (left.astype(jnp.float32) + right.astype(jnp.float32)).astype(jnp.bfloat16)


def sum_three(left, middle, right):
    return left.astype(jnp.float32) + middle.astype(jnp.float32) + right.astype(jnp.float32)


def place_rows(pieces, rows):
    full = jnp.zeros((len(pieces) * rows, pieces[0][0].shape[1]), pieces[0][0].dtype)
    for piece, index in pieces:
        full = lax.dynamic_update_slice(full, piece, (index * rows, 0))
    return full


def first_rows(rows):
    x = lax.axis_index("x")
    z = lax.axis_index("zh")
    return jnp.stack(
        [
            ((((x + dx) % RING) * RING + (z + dz) % RING) * rows + offset).astype(jnp.int32)
            for offset in (0, rows // 2)
            for dx in range(RING)
            for dz in range(RING)
        ]
    )


def at(dx, dz):
    return [(dx % RING) * RING + dz % RING, 0]


def low(dx, dz):
    return [at(dx, dz)[0] + RING * RING, 0]


def first_tokens(rows):
    zl = lax.axis_index("zl")
    core = lax.axis_index("core")
    return jnp.stack(
        [
            ((its_zl * 2 + its_core) * rows).astype(jnp.int32)
            for its_zl, its_core in ((zl, core), (zl, 1 - core), (1 - zl, core), (1 - zl, 1 - core))
        ]
    )


def place_tokens(name, starts, pieces):
    arrays = [piece for piece, _, _ in pieces]
    total = sum(piece.shape[0] for piece in arrays)
    copies = [
        (i, 0, piece.shape[0], 0, [whose, offset]) for i, (piece, whose, offset) in enumerate(pieces)
    ]
    return move(name, starts, arrays, [(total, arrays[0].shape[1])], copies)[0]


def gather_all(starts, token_starts, weight, normed, cotangent, beside):
    rows, columns = weight.shape
    half = rows // 2

    x_before = shift(weight, "x", 1)
    x_after = shift(weight, "x", -1)
    x_across = shift(weight, "x", 2)
    later, starts, token_starts = barrier(weight, starts, token_starts)
    z_before = shift(later, "zh", 1)
    z_after = shift(later, "zh", -1)
    z_before, z_after, x_before, x_after, x_across, normed = barrier(
        z_before, z_after, x_before, x_after, x_across, normed
    )

    sides, z_on, z_back = move(
        "pack_sides",
        starts,
        [z_before, z_after],
        [(2 * rows, columns), (half, columns), (half, columns)],
        [
            (0, 0, half, 1, 0),
            (1, half, half, 2, 0),
            (0, 0, rows, 0, 0),
            (1, 0, rows, 0, rows),
        ],
    )
    part = cotangent.shape[0] // 2
    sides, z_on, z_back, cotangent = barrier(sides, z_on, z_back, cotangent)
    from_before = shift(sides, "x", 1)
    from_after = shift(sides, "x", -1)
    z_top = shift(z_on, "zh", 1)
    z_bottom = shift(z_back, "zh", -1)
    zl_top = shift(cotangent[:part], "zl", 1)
    z_top, z_bottom, from_before, from_after, normed, zl_top, cotangent = barrier(
        z_top, z_bottom, from_before, from_after, normed, zl_top, cotangent
    )

    to_after, to_before = move(
        "pack_across",
        starts,
        [z_top, z_bottom, from_before, from_after],
        [(2 * rows, columns)] * 2,
        [
            (0, 0, half, 0, 0),
            (1, 0, half, 0, half),
            (2, 0, rows, 0, rows),
            (0, 0, half, 1, 0),
            (1, 0, half, 1, half),
            (3, rows, rows, 1, rows),
        ],
    )
    to_after, to_before, normed, cotangent, zl_top = barrier(
        to_after, to_before, normed, cotangent, zl_top
    )
    more_before = shift(to_after, "x", 1)
    more_after = shift(to_before, "x", -1)
    normed_zl = shift(normed, "zl", 1)
    cotangent_core = shift(cotangent, "core", 1)
    both_top = shift(zl_top, "core", 1)
    more_before, more_after, normed_zl, cotangent, cotangent_core, both_top, *beside = barrier(
        more_before, more_after, normed_zl, cotangent, cotangent_core, both_top, *beside
    )

    last_on, last_back = move(
        "pack_last",
        starts,
        [more_before, more_after],
        [(half, columns)] * 2,
        [(0, 0, half, 0, 0), (1, half, half, 1, 0)],
    )
    last_on, last_back, normed_zl, normed, cotangent = barrier(
        last_on, last_back, normed_zl, normed, cotangent
    )
    last_top = shift(last_on, "x", 1)
    last_bottom = shift(last_back, "x", -1)
    normed_both = shift(normed_zl, "core", 1)
    normed_core = shift(normed, "core", 1)
    zl_bottom = shift(cotangent[part:], "zl", 1)
    full_normed = place_tokens(
        "place_normed",
        token_starts,
        [(normed, 0, 0), (normed_core, 1, 0), (normed_zl, 2, 0), (normed_both, 3, 0)],
    )
    last_top, last_bottom, full_normed = barrier(last_top, last_bottom, full_normed)

    (full,) = move(
        "place_weight",
        starts,
        [
            weight,
            z_before,
            z_after,
            x_before,
            x_after,
            x_across,
            from_before,
            from_after,
            z_top,
            z_bottom,
            more_before,
            more_after,
            last_top,
            last_bottom,
        ],
        [(RING * RING * rows, columns)],
        [
            (0, 0, rows, 0, at(0, 0)),
            (1, 0, rows, 0, at(0, -1)),
            (2, 0, rows, 0, at(0, 1)),
            (3, 0, rows, 0, at(-1, 0)),
            (4, 0, rows, 0, at(1, 0)),
            (5, 0, rows, 0, at(2, 0)),
            (6, 0, rows, 0, at(-1, -1)),
            (6, rows, rows, 0, at(-1, 1)),
            (7, 0, rows, 0, at(1, -1)),
            (7, rows, rows, 0, at(1, 1)),
            (8, 0, half, 0, at(0, 2)),
            (9, 0, half, 0, low(0, 2)),
            (10, 0, rows, 0, at(-1, 2)),
            (10, rows, rows, 0, at(2, -1)),
            (11, 0, rows, 0, at(1, 2)),
            (11, rows, rows, 0, at(2, 1)),
            (12, 0, half, 0, at(2, 2)),
            (13, 0, half, 0, low(2, 2)),
        ],
    )
    there = [(cotangent, 0, 0), (cotangent_core, 1, 0), (zl_top, 2, 0), (both_top, 3, 0)]
    return full, full_normed, token_starts, there, zl_bottom, beside


def reduce_core(name, token_starts, part, cuts):
    rows = part.shape[0] // 4
    (leaving,) = combine(
        name + "_leave", token_starts, part, [], [[(rows, 3, 0, []), (rows, 1, 0, [])]]
    )
    firsts = [sum(cuts[:i]) for i in range(len(cuts))]
    return combine(
        name + "_add",
        token_starts,
        part,
        [shift(leaving, "core", 1)],
        [[(cut, 2, first, [(0, first)])] for cut, first in zip(cuts, firsts)]
        + [[(rows, 0, 0, [(0, rows)])]],
    )


def wide(value):
    return value.astype(jnp.float32)


def dot(left, right, dims):
    return lax.dot_general(left, right, (dims, ((), ())), preferred_element_type=jnp.float32)


def per_device(
    hidden,
    norm_gain,
    attn_weight,
    adam_first,
    adam_second,
    cotangent,
    pseudo_grad,
    outer_params,
    outer_moment,
    inner_frag,
):
    own_weight = attn_weight[0, :, 0, :]
    inputs = hidden[0].astype(jnp.float32)
    inverse_rms = lax.rsqrt(jnp.mean(inputs * inputs, axis=-1, keepdims=True) + NORM_EPS)
    normed = (inputs * inverse_rms * norm_gain).astype(jnp.bfloat16)
    summed = lax.psum(pseudo_grad[0].astype(jnp.float32).astype(jnp.bfloat16), "replica").astype(
        jnp.float32
    )
    mean_delta = summed / lax.axis_size("replica")
    new_moment = OUTER_MOMENTUM * outer_moment + mean_delta
    new_outer = outer_params - OUTER_RATE * (mean_delta + OUTER_MOMENTUM * new_moment)
    new_inner = (MIXING * inner_frag[0].astype(jnp.float32) + (1.0 - MIXING) * new_outer).astype(
        jnp.bfloat16
    )
    cosine, sine = rope_tables(4 * normed.shape[0])
    starts = first_rows(own_weight.shape[0])
    full_weight, full_normed, token_starts, there, zl_bottom, beside = gather_all(
        starts,
        first_tokens(normed.shape[0]),
        own_weight,
        normed,
        cotangent[0],
        (new_moment, new_outer, new_inner[None], cosine, sine),
    )
    new_moment, new_outer, new_inner, cosine, sine = beside
    qkv_weight = full_weight[:, :QKV]
    out_weight = full_weight[:, QKV:]
    rows = own_weight.shape[0]
    half = rows // 2
    projected = dot(full_normed, qkv_weight, ((1,), (0,)))
    projected, zl_bottom = barrier(projected, zl_bottom)
    both_bottom = shift(zl_bottom, "core", 1)
    rotated, context = attention_forward(projected, cosine, sine)
    rows = own_weight.shape[0]
    half = rows // 2

    tokens = there[0][0].shape[0]
    context, zl_bottom, both_bottom = barrier(context, zl_bottom, both_bottom)
    full_cotangent = place_tokens(
        "place_cotangent",
        token_starts,
        there + [(zl_bottom, 2, tokens // 2), (both_bottom, 3, tokens // 2)],
    )
    out_part = dot(full_cotangent, context, ((0,), (0,))).astype(jnp.bfloat16)
    to_after, to_before = combine(
        "out_first",
        starts,
        out_part,
        [],
        [
            [(rows, 10, 0, []), (half, 9, 0, [])],
            [(half, 9, half, []), (rows, 11, 0, [])],
        ],
    )
    out_forward = shift(to_after, "x", 1)
    out_backward = shift(to_before, "x", -1)
    d_context = dot(full_cotangent, out_weight, ((1,), (0,))).astype(jnp.bfloat16)
    attended_part = through_weight("attended", context, full_weight, QKV)
    attended_one, attended_two, attended_own = reduce_core(
        "attended", token_starts, attended_part, (32, 96)
    )
    attended_one = shift(attended_one, "zl", 1)
    out_forward, out_backward, attended_one, attended_two, d_context = barrier(
        out_forward, out_backward, attended_one, attended_two, d_context
    )

    to_after, to_before = combine(
        "out_second",
        starts,
        out_part,
        [out_forward, out_backward],
        [
            [
                (rows, 6, 0, [(0, 0)]),
                (half, 5, 0, [(0, rows)]),
                (half, 5, half, []),
                (rows, 7, 0, []),
            ],
            [
                (rows, 14, 0, []),
                (half, 13, 0, []),
                (half, 13, half, [(1, 0)]),
                (rows, 15, 0, [(1, half)]),
            ],
        ],
    )
    to_after, to_before, d_context = barrier(to_after, to_before, d_context)
    out_before = shift(to_after, "x", 1)
    out_after = shift(to_before, "x", -1)
    attended_two = shift(attended_two, "zl", 1)
    d_projected = attention_backward(rotated, d_context, cosine, sine)
    d_partial = through_weight("d_normed", d_projected, full_weight, 0)
    qkv_part = weight_gradient(full_normed, d_projected)
    to_after, to_before = combine(
        "qkv_first",
        starts,
        qkv_part,
        [],
        [
            [(rows, 10, 0, []), (rows, 9, 0, [])],
            [(rows, 8, 0, []), (rows, 11, 0, [])],
        ],
    )
    out_before, out_after, attended_two, to_after, to_before, d_partial = barrier(
        out_before, out_after, attended_two, to_after, to_before, d_partial
    )
    attended_away = jnp.concatenate([attended_one, attended_two])
    forward = shift(to_after, "x", 1)
    backward = shift(to_before, "x", -1)

    d_one, d_two, d_three, d_own = reduce_core("d_normed", token_starts, d_partial, (32, 48, 48))
    d_one = shift(d_one, "zl", 1)
    out_before, out_after, d_two = barrier(out_before, out_after, d_two)
    out_top, out_bottom = combine(
        "out_third",
        starts,
        out_part,
        [out_before, out_after],
        [
            [(half, 2, 0, [(0, 0), (1, 0)])],
            [(half, 2, half, [(0, half), (1, half)])],
        ],
    )
    out_top = shift(out_top, "zh", 1)
    out_bottom = shift(out_bottom, "zh", -1)
    layer_out = sum_three(hidden[0], attended_own, attended_away).astype(jnp.bfloat16)
    forward, backward, out_top, out_bottom, d_one, d_two, d_three, layer_out = barrier(
        forward, backward, out_top, out_bottom, d_one, d_two, d_three, layer_out
    )

    to_after, to_before = combine(
        "qkv_second",
        starts,
        qkv_part,
        [forward, backward],
        [
            [(rows, 6, 0, [(0, 0)]), (rows, 4, 0, [])],
            [(rows, 14, 0, []), (rows, 12, 0, [(1, 0)])],
        ],
    )
    across_before = shift(to_after, "x", 1)
    across_after = shift(to_before, "x", -1)
    out_on, out_back = combine(
        "out_fourth",
        starts,
        out_part,
        [out_before, out_after, out_top, out_bottom],
        [
            [
                (half, 1, 0, [(0, rows), (1, rows), (2, 0)]),
                (half, 1, half, [(0, rows + half), (1, rows + half)]),
            ],
            [
                (half, 3, 0, [(0, 2 * rows), (1, 2 * rows)]),
                (half, 3, half, [(0, 2 * rows + half), (1, 2 * rows + half), (3, 0)]),
            ],
        ],
    )
    out_x_on, out_x_back, out_x_two, out_own = combine(
        "out_own",
        starts,
        out_part,
        [],
        [[(rows, 4, 0, [])], [(rows, 12, 0, [])], [(rows, 8, 0, [])], [(rows, 0, 0, [])]],
    )
    out_came = [shift(out_on, "zh", 1), shift(out_back, "zh", -1)]
    d_two = shift(d_two, "zl", 1)
    across_before, across_after, d_two, d_three, out_x_on, out_x_back, out_x_two, *out_came = barrier(
        across_before, across_after, d_two, d_three, out_x_on, out_x_back, out_x_two, *out_came
    )

    top, bottom, to_after, to_before = combine(
        "qkv_third",
        starts,
        qkv_part,
        [forward, backward, across_before, across_after],
        [
            [(half, 2, 0, [(2, 0), (3, 0)])],
            [(half, 2, half, [(2, half), (3, half)])],
            [(rows, 5, 0, [(0, rows)]), (rows, 7, 0, [])],
            [(rows, 13, 0, []), (rows, 15, 0, [(1, rows)])],
        ],
    )
    sides_before = shift(to_after, "x", 1)
    sides_after = shift(to_before, "x", -1)
    top = shift(top, "zh", 1)
    bottom = shift(bottom, "zh", -1)
    d_three = shift(d_three, "zl", 1)
    top, bottom, sides_before, sides_after, d_three, out_x_on, out_x_back, out_x_two = barrier(
        top, bottom, sides_before, sides_after, d_three, out_x_on, out_x_back, out_x_two
    )

    z_on, z_back = combine(
        "qkv_fourth",
        starts,
        qkv_part,
        [sides_before, sides_after, top, bottom],
        [
            [
                (half, 1, 0, [(0, 0), (1, 0), (2, 0)]),
                (half, 1, half, [(0, half), (1, half)]),
            ],
            [
                (half, 3, 0, [(0, rows), (1, rows)]),
                (half, 3, half, [(0, rows + half), (1, rows + half), (3, 0)]),
            ],
        ],
    )
    z_on = shift(z_on, "zh", 1)
    z_back = shift(z_back, "zh", -1)
    out_came += [
        shift(out_x_on, "x", 1),
        shift(out_x_back, "x", -1),
        shift(out_x_two, "x", 2),
    ]
    (qkv_own,) = combine(
        "qkv_own",
        starts,
        qkv_part,
        [across_before, across_after],
        [[(rows, 0, 0, [(0, rows), (1, rows)])]],
    )
    qkv_came = [z_on, z_back]
    d_normed = wide(d_own) + wide(jnp.concatenate([d_one, d_two, d_three]))
    scaled = d_normed * norm_gain
    d_inputs = inverse_rms * scaled - inputs * inverse_rms**3 * jnp.mean(
        inputs * scaled, axis=-1, keepdims=True
    )
    hidden_grad = (cotangent[0].astype(jnp.float32) + d_inputs).astype(jnp.bfloat16)
    flat = (-1, 128)
    new_weight, first_new, second_new = adam_step(
        qkv_own,
        out_own,
        qkv_came,
        out_came,
        own_weight,
        adam_first.reshape(flat),
        adam_second.reshape(flat),
    )
    new_weight = new_weight.reshape(attn_weight.shape)
    first_new = first_new.reshape(adam_first.shape)
    second_new = second_new.reshape(adam_second.shape)
    return (
        layer_out[None],
        hidden_grad[None],
        new_weight,
        first_new,
        second_new,
        new_outer,
        new_moment,
        new_inner,
    )


def solution(mesh):
    fine = Mesh(mesh.devices.reshape(4, 4, 4, 2, 2), ("replica", "x", "zh", "zl", "core"))
    rows = ("x", "zh", "zl", "core")
    tokens = P("replica", rows, None)
    weights = P("replica", ("x", "zh"), ("zl", "core"), None)
    fragment = P("replica", rows)
    return jax.shard_map(
        per_device,
        mesh=fine,
        in_specs=(
            tokens,
            P(),
            weights,
            weights,
            weights,
            tokens,
            fragment,
            P(rows),
            P(rows),
            fragment,
        ),
        out_specs=(
            tokens,
            tokens,
            weights,
            weights,
            weights,
            P(rows),
            P(rows),
            fragment,
        ),
        check_vma=False,
    )
```

```python
import functools
import math

import jax
import jax.numpy as jnp
from jax import lax
from jax.experimental import pallas as pl
from jax.experimental.pallas import tpu as pltpu
from jax.sharding import Mesh, PartitionSpec as P

HQ = 16
HK = 4
HD = 128
GROUP = HQ // HK
QKV = (GROUP + 2) * HD


ROPE_BASE = 500000.0
NORM_EPS = 1e-05
LEARN_RATE = 0.001
BETA_ONE = 0.9
BETA_TWO = 0.95
ADAM_EPS = 1e-08
DECAY = 0.1
CORRECT_ONE = 0.9999734386011124
CORRECT_TWO = 0.994079470779666
OUTER_RATE = 0.7
OUTER_MOMENTUM = 0.9
MIXING = 0.5

RING = 4


def rope_tables(length):
    positions = jnp.arange(length, dtype=jnp.float32)
    freqs = ROPE_BASE ** (-2.0 * jnp.arange(HD // 2, dtype=jnp.float32) / HD)
    angles = positions[:, None] * freqs[None, :]
    cosine, sine = jnp.cos(angles), jnp.sin(angles)
    return (
        jnp.concatenate([cosine, cosine], axis=-1),
        jnp.concatenate([-sine, sine], axis=-1),
    )


TILE = 256
SCALE = 1.0 / math.sqrt(HD)


def swap_turn(values, cosine, sine):
    return values * cosine + pltpu.roll(values, HD // 2, 1) * sine


def mm(left, right, dims):
    return lax.dot_general(left, right, (dims, ((), ())), preferred_element_type=jnp.float32)


def tile_probabilities(queries, keys, place):
    scores = mm(queries, keys, ((1,), (1,))) * SCALE
    rows = lax.broadcasted_iota(jnp.int32, scores.shape, 0) + place * TILE
    columns = lax.broadcasted_iota(jnp.int32, scores.shape, 1)
    scores = jnp.where(rows >= columns, scores, -jnp.inf)
    exponent = jnp.exp(scores - jnp.max(scores, axis=-1, keepdims=True))
    return exponent / jnp.sum(exponent, axis=-1, keepdims=True)


def forward_kernel(projected, cosine, sine, rotated, context):
    cos = cosine[...]
    sin = sine[...]
    for head in range(GROUP + 1):
        part = pl.ds(head * HD, HD)
        rotated[:, part] = swap_turn(projected[:, part], cos, sin).astype(jnp.bfloat16)
    part = pl.ds((GROUP + 1) * HD, HD)
    rotated[:, part] = projected[:, part].astype(jnp.bfloat16)
    for place in range(projected.shape[0] // TILE):
        rows = pl.ds(place * TILE, TILE)
        known = pl.ds(0, (place + 1) * TILE)
        keys = rotated[known, pl.ds(GROUP * HD, HD)]
        values = rotated[known, pl.ds((GROUP + 1) * HD, HD)]
        for head in range(GROUP):
            part = pl.ds(head * HD, HD)
            probs = tile_probabilities(rotated[rows, part], keys, place).astype(jnp.bfloat16)
            context[rows, part] = mm(probs, values, ((1,), (0,))).astype(jnp.bfloat16)


def backward_kernel(rotated, d_context, cosine, sine, d_projected, d_keys, d_values):
    d_keys[...] = jnp.zeros_like(d_keys)
    d_values[...] = jnp.zeros_like(d_values)
    for place in range(rotated.shape[0] // TILE):
        rows = pl.ds(place * TILE, TILE)
        known = pl.ds(0, (place + 1) * TILE)
        keys = rotated[known, pl.ds(GROUP * HD, HD)]
        values = rotated[known, pl.ds((GROUP + 1) * HD, HD)]
        cos = cosine[rows, :]
        sin = sine[rows, :]
        for head in range(GROUP):
            part = pl.ds(head * HD, HD)
            queries = rotated[rows, part]
            upstream = d_context[rows, part]
            probs = tile_probabilities(queries, keys, place)
            d_probs = mm(upstream, values, ((1,), (1,)))
            d_values[known, :] += mm(probs.astype(jnp.bfloat16), upstream, ((0,), (0,)))
            d_scores = probs * (d_probs - jnp.sum(d_probs * probs, axis=-1, keepdims=True))
            d_scores = (d_scores * SCALE).astype(jnp.bfloat16)
            d_keys[known, :] += mm(d_scores, queries, ((0,), (0,)))
            d_queries = mm(d_scores, keys, ((1,), (0,)))
            d_projected[rows, part] = swap_turn(d_queries, cos, -sin).astype(jnp.bfloat16)
    d_projected[:, pl.ds(GROUP * HD, HD)] = swap_turn(
        d_keys[...], cosine[...], -sine[...]
    ).astype(jnp.bfloat16)
    d_projected[:, pl.ds((GROUP + 1) * HD, HD)] = d_values[...].astype(jnp.bfloat16)


def attention_forward(projected, cosine, sine):
    length = projected.shape[0]
    return pl.pallas_call(
        forward_kernel,
        out_shape=(
            jax.ShapeDtypeStruct((length, QKV), jnp.bfloat16),
            jax.ShapeDtypeStruct((length, GROUP * HD), jnp.bfloat16),
        ),
        cost_estimate=LIGHT,
        compiler_params=pltpu.CompilerParams(vmem_limit_bytes=16 << 20),
        name="attention_forward",
    )(projected, cosine, sine)


def attention_backward(rotated, d_context, cosine, sine):
    length = rotated.shape[0]
    return pl.pallas_call(
        backward_kernel,
        out_shape=jax.ShapeDtypeStruct((length, QKV), jnp.bfloat16),
        scratch_shapes=[
            pltpu.VMEM((length, HD), jnp.float32),
            pltpu.VMEM((length, HD), jnp.float32),
        ],
        cost_estimate=LIGHT,
        compiler_params=pltpu.CompilerParams(vmem_limit_bytes=16 << 20),
        name="attention_backward",
    )(rotated, d_context, cosine, sine)


ADAM_ROWS = 64


def adam_kernel(n_qkv, qkv_block, out_block, *refs):
    weight, first, second, new_weight, new_first, new_second = refs[-6:]
    qkv_came = (qkv_block,) + refs[:n_qkv]
    out_came = (out_block,) + refs[n_qkv:-6]
    blocks = weight.shape[1] // 128
    for place in range(blocks):
        part = pl.ds(place * 128, 128)
        if place < QKV // 128:
            terms = [ref[:, part].astype(jnp.float32) for ref in qkv_came]
        else:
            out_columns = pl.ds(place * 128 - QKV, 128)
            terms = [ref[:, out_columns].astype(jnp.float32) for ref in out_came]
        gradient = sum(terms[1:], terms[0])
        rows = pl.ds(place, weight.shape[0], stride=blocks)
        first_new = BETA_ONE * first[rows, :] + (1.0 - BETA_ONE) * gradient
        second_new = BETA_TWO * second[rows, :] + (1.0 - BETA_TWO) * gradient * gradient
        weight_wide = weight[:, part].astype(jnp.float32)
        update = (
            first_new / CORRECT_ONE / (jnp.sqrt(second_new / CORRECT_TWO) + ADAM_EPS)
            + DECAY * weight_wide
        )
        new_weight[:, part] = (weight_wide - LEARN_RATE * update).astype(jnp.bfloat16)
        new_first[rows, :] = first_new
        new_second[rows, :] = second_new


def adam_step(qkv_own, out_own, qkv_came, out_came, weight, first, second):
    rows, columns = weight.shape
    blocks = columns // 128
    steps = rows // ADAM_ROWS

    def spec(shape):
        return pl.BlockSpec(shape, lambda i: (i, 0))

    block = spec((ADAM_ROWS, columns))
    moment = spec((ADAM_ROWS * blocks, 128))
    moments = jax.ShapeDtypeStruct((rows * blocks, 128), jnp.float32)
    qkv_spec = spec((ADAM_ROWS, QKV))
    out_spec = spec((ADAM_ROWS, columns - QKV))
    return pl.pallas_call(
        functools.partial(adam_kernel, len(qkv_came)),
        grid=(steps,),
        in_specs=[qkv_spec, out_spec]
        + [qkv_spec] * len(qkv_came)
        + [out_spec] * len(out_came)
        + [block, moment, moment],
        out_specs=(block, moment, moment),
        out_shape=(jax.ShapeDtypeStruct((rows, columns), jnp.bfloat16), moments, moments),
        cost_estimate=pl.CostEstimate(
            flops=20 * rows * columns, bytes_accessed=32 * rows * columns, transcendentals=0
        ),
        compiler_params=pltpu.CompilerParams(vmem_limit_bytes=24 << 20),
        name="adam",
    )(qkv_own, out_own, *qkv_came, *out_came, weight, first, second)


SMEM = pl.BlockSpec(memory_space=pltpu.SMEM)
VMEM = pl.BlockSpec(memory_space=pltpu.VMEM)
LIGHT = pl.CostEstimate(flops=0, bytes_accessed=0, transcendentals=0)


def call_rows(name, kernel, starts, operands, shapes):
    held = 4 * sum(rows * columns for rows, columns in shapes)
    return pl.pallas_call(
        kernel,
        in_specs=[SMEM] + [VMEM] * len(operands),
        out_shape=[jax.ShapeDtypeStruct(shape, jnp.bfloat16) for shape in shapes],
        cost_estimate=LIGHT,
        compiler_params=pltpu.CompilerParams(vmem_limit_bytes=(4 << 20) + held),
        name=name,
    )(starts, *operands)


def move(name, starts, sources, shapes, copies):
    def kernel(starts, *refs):
        for source, from_row, rows, target, to_row in copies:
            if isinstance(to_row, list):
                place, offset = to_row
                to_row = pl.multiple_of(starts[place] + offset, math.gcd(128, offset))
            target = refs[len(sources) + target]
            target[pl.ds(to_row, rows), :] = refs[source][pl.ds(from_row, rows), :]

    return call_rows(name, kernel, starts, sources, shapes)


def combine(name, starts, part, came, outputs):
    columns = part.shape[1]

    def kernel(starts, part, *refs):
        for target, segs in zip(refs[len(came) :], outputs):
            to_row = 0
            for rows, block, offset, terms in segs:
                first = pl.multiple_of(starts[block] + offset, math.gcd(128, offset))
                total = part[pl.ds(first, rows), :]
                if terms:
                    total = total.astype(jnp.float32)
                    for array, row in terms:
                        total = total + refs[array][pl.ds(row, rows), :].astype(jnp.float32)
                target[pl.ds(to_row, rows), :] = total.astype(jnp.bfloat16)
                to_row += rows

    shapes = [(sum(seg[0] for seg in segs), columns) for segs in outputs]
    return call_rows(name, kernel, starts, [part, *came], shapes)


BLOCK = 512


def product(name, kernel, shape, *operands):
    return pl.pallas_call(
        kernel,
        in_specs=[VMEM] * len(operands),
        out_shape=jax.ShapeDtypeStruct(shape, jnp.bfloat16),
        cost_estimate=LIGHT,
        compiler_params=pltpu.CompilerParams(vmem_limit_bytes=24 << 20),
        name=name,
    )(*operands)


def weight_gradient(tokens, upstream):
    model = tokens.shape[1]

    def kernel(tokens, upstream, gradient):
        right = upstream[...]
        for first in range(0, model, BLOCK):
            part = pl.ds(first, BLOCK)
            block = mm(tokens[:, part], right, ((0,), (0,)))
            gradient[part, :] = block.astype(jnp.bfloat16)

    return product("weight_gradient", kernel, (model, upstream.shape[1]), tokens, upstream)


def through_weight(name, left, weight, column):
    length, columns = left.shape
    model = weight.shape[0]

    def kernel(left, weight, total):
        rows = left[...]
        for first in range(0, model, BLOCK):
            part = pl.ds(first, BLOCK)
            block = mm(rows, weight[part, pl.ds(column, columns)], ((1,), (1,)))
            total[:, part] = block.astype(jnp.bfloat16)

    return product(name, kernel, (length, model), left, weight)


def shift(value, axis, step):
    size = lax.axis_size(axis)
    return lax.ppermute(value, axis, [(i, (i + step) % size) for i in range(size)])


def barrier(*values):
    return lax.optimization_barrier(values)


def add(left, right):
    return (left.astype(jnp.float32) + right.astype(jnp.float32)).astype(jnp.bfloat16)


def sum_three(left, middle, right):
    return left.astype(jnp.float32) + middle.astype(jnp.float32) + right.astype(jnp.float32)


def place_rows(pieces, rows):
    full = jnp.zeros((len(pieces) * rows, pieces[0][0].shape[1]), pieces[0][0].dtype)
    for piece, index in pieces:
        full = lax.dynamic_update_slice(full, piece, (index * rows, 0))
    return full


def first_rows(rows):
    x = lax.axis_index("x")
    z = lax.axis_index("zh")
    return jnp.stack(
        [
            ((((x + dx) % RING) * RING + (z + dz) % RING) * rows + offset).astype(jnp.int32)
            for offset in (0, rows // 2)
            for dx in range(RING)
            for dz in range(RING)
        ]
    )


def at(dx, dz):
    return [(dx % RING) * RING + dz % RING, 0]


def low(dx, dz):
    return [at(dx, dz)[0] + RING * RING, 0]


def first_tokens(rows):
    zl = lax.axis_index("zl")
    core = lax.axis_index("core")
    return jnp.stack(
        [
            ((its_zl * 2 + its_core) * rows).astype(jnp.int32)
            for its_zl, its_core in ((zl, core), (zl, 1 - core), (1 - zl, core), (1 - zl, 1 - core))
        ]
    )


def place_tokens(name, starts, pieces):
    arrays = [piece for piece, _, _ in pieces]
    total = sum(piece.shape[0] for piece in arrays)
    copies = [
        (i, 0, piece.shape[0], 0, [whose, offset]) for i, (piece, whose, offset) in enumerate(pieces)
    ]
    return move(name, starts, arrays, [(total, arrays[0].shape[1])], copies)[0]


def gather_all(starts, token_starts, weight, normed, cotangent, beside, delta, outer_step):
    rows, columns = weight.shape
    half = rows // 2

    x_before = shift(weight, "x", 1)
    x_after = shift(weight, "x", -1)
    x_across = shift(weight, "x", 2)
    later, starts, token_starts = barrier(weight, starts, token_starts)
    z_before = shift(later, "zh", 1)
    z_after = shift(later, "zh", -1)
    z_before, z_after, x_before, x_after, x_across, normed, delta = barrier(
        z_before, z_after, x_before, x_after, x_across, normed, delta
    )

    sides, z_on, z_back = move(
        "pack_sides",
        starts,
        [z_before, z_after],
        [(2 * rows, columns), (half, columns), (half, columns)],
        [
            (0, 0, half, 1, 0),
            (1, half, half, 2, 0),
            (0, 0, rows, 0, 0),
            (1, 0, rows, 0, rows),
        ],
    )
    part = cotangent.shape[0] // 2
    sides, z_on, z_back, cotangent = barrier(sides, z_on, z_back, cotangent)
    from_before = shift(sides, "x", 1)
    from_after = shift(sides, "x", -1)
    z_top = shift(z_on, "zh", 1)
    z_bottom = shift(z_back, "zh", -1)
    zl_top = shift(cotangent[:part], "zl", 1)
    z_top, z_bottom, from_before, from_after, normed, zl_top, cotangent, delta = barrier(
        z_top, z_bottom, from_before, from_after, normed, zl_top, cotangent, delta
    )
    deltas = [shift(delta, "replica", step) for step in (1, -1, 2)]

    to_after, to_before = move(
        "pack_across",
        starts,
        [z_top, z_bottom, from_before, from_after],
        [(2 * rows, columns)] * 2,
        [
            (0, 0, half, 0, 0),
            (1, 0, half, 0, half),
            (2, 0, rows, 0, rows),
            (0, 0, half, 1, 0),
            (1, 0, half, 1, half),
            (3, rows, rows, 1, rows),
        ],
    )
    to_after, to_before, normed, cotangent, zl_top = barrier(
        to_after, to_before, normed, cotangent, zl_top
    )
    more_before = shift(to_after, "x", 1)
    more_after = shift(to_before, "x", -1)
    normed_zl = shift(normed, "zl", 1)
    cotangent_core = shift(cotangent, "core", 1)
    both_top = shift(zl_top, "core", 1)
    more_before, more_after, normed_zl, cotangent, cotangent_core, both_top, *deltas = barrier(
        more_before, more_after, normed_zl, cotangent, cotangent_core, both_top, *deltas
    )
    beside = (*outer_step(delta, deltas), *beside)

    last_on, last_back = move(
        "pack_last",
        starts,
        [more_before, more_after],
        [(half, columns)] * 2,
        [(0, 0, half, 0, 0), (1, half, half, 1, 0)],
    )
    last_on, last_back, normed_zl, normed, cotangent = barrier(
        last_on, last_back, normed_zl, normed, cotangent
    )
    last_top = shift(last_on, "x", 1)
    last_bottom = shift(last_back, "x", -1)
    normed_both = shift(normed_zl, "core", 1)
    normed_core = shift(normed, "core", 1)
    zl_bottom = shift(cotangent[part:], "zl", 1)
    full_normed = place_tokens(
        "place_normed",
        token_starts,
        [(normed, 0, 0), (normed_core, 1, 0), (normed_zl, 2, 0), (normed_both, 3, 0)],
    )
    last_top, last_bottom, full_normed, *beside = barrier(
        last_top, last_bottom, full_normed, *beside
    )

    (full,) = move(
        "place_weight",
        starts,
        [
            weight,
            z_before,
            z_after,
            x_before,
            x_after,
            x_across,
            from_before,
            from_after,
            z_top,
            z_bottom,
            more_before,
            more_after,
            last_top,
            last_bottom,
        ],
        [(RING * RING * rows, columns)],
        [
            (0, 0, rows, 0, at(0, 0)),
            (1, 0, rows, 0, at(0, -1)),
            (2, 0, rows, 0, at(0, 1)),
            (3, 0, rows, 0, at(-1, 0)),
            (4, 0, rows, 0, at(1, 0)),
            (5, 0, rows, 0, at(2, 0)),
            (6, 0, rows, 0, at(-1, -1)),
            (6, rows, rows, 0, at(-1, 1)),
            (7, 0, rows, 0, at(1, -1)),
            (7, rows, rows, 0, at(1, 1)),
            (8, 0, half, 0, at(0, 2)),
            (9, 0, half, 0, low(0, 2)),
            (10, 0, rows, 0, at(-1, 2)),
            (10, rows, rows, 0, at(2, -1)),
            (11, 0, rows, 0, at(1, 2)),
            (11, rows, rows, 0, at(2, 1)),
            (12, 0, half, 0, at(2, 2)),
            (13, 0, half, 0, low(2, 2)),
        ],
    )
    there = [(cotangent, 0, 0), (cotangent_core, 1, 0), (zl_top, 2, 0), (both_top, 3, 0)]
    return full, full_normed, token_starts, there, zl_bottom, beside


def reduce_core(name, token_starts, part, cuts):
    rows = part.shape[0] // 4
    (leaving,) = combine(
        name + "_leave", token_starts, part, [], [[(rows, 3, 0, []), (rows, 1, 0, [])]]
    )
    firsts = [sum(cuts[:i]) for i in range(len(cuts))]
    return combine(
        name + "_add",
        token_starts,
        part,
        [shift(leaving, "core", 1)],
        [[(cut, 2, first, [(0, first)])] for cut, first in zip(cuts, firsts)]
        + [[(rows, 0, 0, [(0, rows)])]],
    )


def wide(value):
    return value.astype(jnp.float32)


def dot(left, right, dims):
    return lax.dot_general(left, right, (dims, ((), ())), preferred_element_type=jnp.float32)


def per_device(
    hidden,
    norm_gain,
    attn_weight,
    adam_first,
    adam_second,
    cotangent,
    pseudo_grad,
    outer_params,
    outer_moment,
    inner_frag,
):
    own_weight = attn_weight[0, :, 0, :]
    inputs = hidden[0].astype(jnp.float32)
    inverse_rms = lax.rsqrt(jnp.mean(inputs * inputs, axis=-1, keepdims=True) + NORM_EPS)
    normed = (inputs * inverse_rms * norm_gain).astype(jnp.bfloat16)
    def outer_step(delta, came):
        mean_delta = sum([wide(part) for part in came], wide(delta)) / lax.axis_size("replica")
        new_moment = OUTER_MOMENTUM * outer_moment + mean_delta
        new_outer = outer_params - OUTER_RATE * (mean_delta + OUTER_MOMENTUM * new_moment)
        mixed = MIXING * inner_frag[0].astype(jnp.float32) + (1.0 - MIXING) * new_outer
        return new_moment, new_outer, mixed.astype(jnp.bfloat16)[None]

    cosine, sine = rope_tables(4 * normed.shape[0])
    starts = first_rows(own_weight.shape[0])
    full_weight, full_normed, token_starts, there, zl_bottom, beside = gather_all(
        starts,
        first_tokens(normed.shape[0]),
        own_weight,
        normed,
        cotangent[0],
        (cosine, sine),
        pseudo_grad[0],
        outer_step,
    )
    new_moment, new_outer, new_inner, cosine, sine = beside
    qkv_weight = full_weight[:, :QKV]
    out_weight = full_weight[:, QKV:]
    rows = own_weight.shape[0]
    half = rows // 2
    projected = dot(full_normed, qkv_weight, ((1,), (0,)))
    projected, zl_bottom = barrier(projected, zl_bottom)
    both_bottom = shift(zl_bottom, "core", 1)
    rotated, context = attention_forward(projected, cosine, sine)
    rows = own_weight.shape[0]
    half = rows // 2

    tokens = there[0][0].shape[0]
    context, zl_bottom, both_bottom = barrier(context, zl_bottom, both_bottom)
    full_cotangent = place_tokens(
        "place_cotangent",
        token_starts,
        there + [(zl_bottom, 2, tokens // 2), (both_bottom, 3, tokens // 2)],
    )
    out_part = dot(full_cotangent, context, ((0,), (0,))).astype(jnp.bfloat16)
    to_after, to_before = combine(
        "out_first",
        starts,
        out_part,
        [],
        [
            [(rows, 10, 0, []), (half, 9, 0, [])],
            [(half, 9, half, []), (rows, 11, 0, [])],
        ],
    )
    out_forward = shift(to_after, "x", 1)
    out_backward = shift(to_before, "x", -1)
    d_context = dot(full_cotangent, out_weight, ((1,), (0,))).astype(jnp.bfloat16)
    attended_part = through_weight("attended", context, full_weight, QKV)
    attended_one, attended_two, attended_own = reduce_core(
        "attended", token_starts, attended_part, (32, 96)
    )
    attended_one = shift(attended_one, "zl", 1)
    out_forward, out_backward, attended_one, attended_two, d_context = barrier(
        out_forward, out_backward, attended_one, attended_two, d_context
    )

    to_after, to_before = combine(
        "out_second",
        starts,
        out_part,
        [out_forward, out_backward],
        [
            [
                (rows, 6, 0, [(0, 0)]),
                (half, 5, 0, [(0, rows)]),
                (half, 5, half, []),
                (rows, 7, 0, []),
            ],
            [
                (rows, 14, 0, []),
                (half, 13, 0, []),
                (half, 13, half, [(1, 0)]),
                (rows, 15, 0, [(1, half)]),
            ],
        ],
    )
    to_after, to_before, d_context = barrier(to_after, to_before, d_context)
    out_before = shift(to_after, "x", 1)
    out_after = shift(to_before, "x", -1)
    attended_two = shift(attended_two, "zl", 1)
    d_projected = attention_backward(rotated, d_context, cosine, sine)
    d_partial = through_weight("d_normed", d_projected, full_weight, 0)
    qkv_part = weight_gradient(full_normed, d_projected)
    to_after, to_before = combine(
        "qkv_first",
        starts,
        qkv_part,
        [],
        [
            [(rows, 10, 0, []), (rows, 9, 0, [])],
            [(rows, 8, 0, []), (rows, 11, 0, [])],
        ],
    )
    out_before, out_after, attended_two, to_after, to_before, d_partial = barrier(
        out_before, out_after, attended_two, to_after, to_before, d_partial
    )
    attended_away = jnp.concatenate([attended_one, attended_two])
    forward = shift(to_after, "x", 1)
    backward = shift(to_before, "x", -1)

    d_one, d_two, d_three, d_own = reduce_core("d_normed", token_starts, d_partial, (32, 48, 48))
    d_one = shift(d_one, "zl", 1)
    out_before, out_after, d_two = barrier(out_before, out_after, d_two)
    out_top, out_bottom = combine(
        "out_third",
        starts,
        out_part,
        [out_before, out_after],
        [
            [(half, 2, 0, [(0, 0), (1, 0)])],
            [(half, 2, half, [(0, half), (1, half)])],
        ],
    )
    out_top = shift(out_top, "zh", 1)
    out_bottom = shift(out_bottom, "zh", -1)
    layer_out = sum_three(hidden[0], attended_own, attended_away).astype(jnp.bfloat16)
    forward, backward, out_top, out_bottom, d_one, d_two, d_three, layer_out = barrier(
        forward, backward, out_top, out_bottom, d_one, d_two, d_three, layer_out
    )

    to_after, to_before = combine(
        "qkv_second",
        starts,
        qkv_part,
        [forward, backward],
        [
            [(rows, 6, 0, [(0, 0)]), (rows, 4, 0, [])],
            [(rows, 14, 0, []), (rows, 12, 0, [(1, 0)])],
        ],
    )
    across_before = shift(to_after, "x", 1)
    across_after = shift(to_before, "x", -1)
    out_on, out_back = combine(
        "out_fourth",
        starts,
        out_part,
        [out_before, out_after, out_top, out_bottom],
        [
            [
                (half, 1, 0, [(0, rows), (1, rows), (2, 0)]),
                (half, 1, half, [(0, rows + half), (1, rows + half)]),
            ],
            [
                (half, 3, 0, [(0, 2 * rows), (1, 2 * rows)]),
                (half, 3, half, [(0, 2 * rows + half), (1, 2 * rows + half), (3, 0)]),
            ],
        ],
    )
    out_x_on, out_x_back, out_x_two, out_own = combine(
        "out_own",
        starts,
        out_part,
        [],
        [[(rows, 4, 0, [])], [(rows, 12, 0, [])], [(rows, 8, 0, [])], [(rows, 0, 0, [])]],
    )
    out_came = [shift(out_on, "zh", 1), shift(out_back, "zh", -1)]
    d_two = shift(d_two, "zl", 1)
    across_before, across_after, d_two, d_three, out_x_on, out_x_back, out_x_two, *out_came = barrier(
        across_before, across_after, d_two, d_three, out_x_on, out_x_back, out_x_two, *out_came
    )

    top, bottom, to_after, to_before = combine(
        "qkv_third",
        starts,
        qkv_part,
        [forward, backward, across_before, across_after],
        [
            [(half, 2, 0, [(2, 0), (3, 0)])],
            [(half, 2, half, [(2, half), (3, half)])],
            [(rows, 5, 0, [(0, rows)]), (rows, 7, 0, [])],
            [(rows, 13, 0, []), (rows, 15, 0, [(1, rows)])],
        ],
    )
    sides_before = shift(to_after, "x", 1)
    sides_after = shift(to_before, "x", -1)
    top = shift(top, "zh", 1)
    bottom = shift(bottom, "zh", -1)
    d_three = shift(d_three, "zl", 1)
    top, bottom, sides_before, sides_after, d_three, out_x_on, out_x_back, out_x_two = barrier(
        top, bottom, sides_before, sides_after, d_three, out_x_on, out_x_back, out_x_two
    )

    z_on, z_back = combine(
        "qkv_fourth",
        starts,
        qkv_part,
        [sides_before, sides_after, top, bottom],
        [
            [
                (half, 1, 0, [(0, 0), (1, 0), (2, 0)]),
                (half, 1, half, [(0, half), (1, half)]),
            ],
            [
                (half, 3, 0, [(0, rows), (1, rows)]),
                (half, 3, half, [(0, rows + half), (1, rows + half), (3, 0)]),
            ],
        ],
    )
    z_on = shift(z_on, "zh", 1)
    z_back = shift(z_back, "zh", -1)
    out_came += [
        shift(out_x_on, "x", 1),
        shift(out_x_back, "x", -1),
        shift(out_x_two, "x", 2),
    ]
    (qkv_own,) = combine(
        "qkv_own",
        starts,
        qkv_part,
        [across_before, across_after],
        [[(rows, 0, 0, [(0, rows), (1, rows)])]],
    )
    qkv_came = [z_on, z_back]
    d_normed = wide(d_own) + wide(jnp.concatenate([d_one, d_two, d_three]))
    scaled = d_normed * norm_gain
    d_inputs = inverse_rms * scaled - inputs * inverse_rms**3 * jnp.mean(
        inputs * scaled, axis=-1, keepdims=True
    )
    hidden_grad = (cotangent[0].astype(jnp.float32) + d_inputs).astype(jnp.bfloat16)
    flat = (-1, 128)
    new_weight, first_new, second_new = adam_step(
        qkv_own,
        out_own,
        qkv_came,
        out_came,
        own_weight,
        adam_first.reshape(flat),
        adam_second.reshape(flat),
    )
    new_weight = new_weight.reshape(attn_weight.shape)
    first_new = first_new.reshape(adam_first.shape)
    second_new = second_new.reshape(adam_second.shape)
    return (
        layer_out[None],
        hidden_grad[None],
        new_weight,
        first_new,
        second_new,
        new_outer,
        new_moment,
        new_inner,
    )


def solution(mesh):
    fine = Mesh(mesh.devices.reshape(4, 4, 4, 2, 2), ("replica", "x", "zh", "zl", "core"))
    rows = ("x", "zh", "zl", "core")
    tokens = P("replica", rows, None)
    weights = P("replica", ("x", "zh"), ("zl", "core"), None)
    fragment = P("replica", rows)
    return jax.shard_map(
        per_device,
        mesh=fine,
        in_specs=(
            tokens,
            P(),
            weights,
            weights,
            weights,
            tokens,
            fragment,
            P(rows),
            P(rows),
            fragment,
        ),
        out_specs=(
            tokens,
            tokens,
            weights,
            weights,
            weights,
            P(rows),
            P(rows),
            fragment,
        ),
        check_vma=False,
    )
```
